128 devices in a mesh: fsdp: 32 (over y, x, core), dp: 4 (over z).
Axes of the slice: x: 4, y: 4, z: 4, core: 2. Of those that a mesh axis runs over, the one named last changes fastest.
Arguments:
- grad_parts: float32 [4, 32, 768, 4096], P('dp', None, None, 'fsdp'), may hold values from -6 to 6
- master: float32 [32, 768, 4096], P(None, 'dp', 'fsdp'), may hold values from -0.21875 to 0.21875
- moment_one: float32 [32, 768, 4096], P(None, 'dp', 'fsdp'), may hold values from -1.2 to 1.2
- moment_two: float32 [32, 768, 4096], P(None, 'dp', 'fsdp'), may hold values from 0.05 to 0.5
- gate_owned: bfloat16 [32, 768, 4096], P('fsdp', 'dp'), may hold values from -0.09375 to 0.09375
- up_owned: bfloat16 [32, 768, 4096], P('fsdp', 'dp'), may hold values from -0.09375 to 0.09375
- tokens: bfloat16 [1024, 4096], P(('fsdp', 'dp')), may hold values from -6 to 6
- expert_ids: int32 [1024, 8], P(('fsdp', 'dp')), may hold values from 0 to 31, all different within a row; in each aligned block of 8 rows (0 to 7, 8 to 15, ...) at most 4 rows name the same one
- gate_values: float32 [1024, 8], P(('fsdp', 'dp')), may hold values from 0.05 to 1
- owner_map: int32 [32], replicated, may hold values from 0 to 31, each once
Outputs:
- owned_down: bfloat16 [32, 768, 4096], P('fsdp', 'dp')
- combined: bfloat16 [1024, 4096], P(('fsdp', 'dp'))
The draws below stay inside these ranges and needn't reach their ends.
Inputs may be any that keep to these rules, and one draw needn't show every extreme that they name: `expert_ids`: each row names 8 different experts. In each aligned block of 8 rows (the rows of one device) no expert is named by more than 4 rows, a bound that some block reaches. A permutation: expert e is held by index owner_map[e] of fsdp.
All inputs are finite; a program needn't handle non-finite values.
Results may differ from the reference program's by a relative error of at most 0.007.
Values may be sent and summed in bfloat16 or wider, within the bound.
A program may use at most 128 MiB of HBM per device.

```python
import math
import jax
import jax.numpy as jnp
import numpy as np
from jax import lax

D = 4096
FF_W = 768
TOP = 8
TOK_DEV = 8
EXPERTS = 32
CAP = 4
TOKENS = 1024
N_FSDP = 32
N_DP = 4


def strengthened(result, stream_key, source, target, shards_of, factor):
    owner, partner = [(jnp.arange(result.shape[dim]) // (result.shape[dim] // shards_of)).reshape([-1 if axis == dim else 1 for axis in range(result.ndim)]) for dim in (source, target)]
    chosen = jax.random.permutation(stream_key, shards_of)[partner]
    strong = (owner == chosen) | (owner == (partner + shards_of // 2) % shards_of)
    return jnp.where(strong, factor * result, result)


def block_scale(rng, shape, split, smallest, high):
    def one(axis_at, parts):
        draws = jax.random.uniform(jax.random.fold_in(jax.random.fold_in(rng, 6), axis_at), (parts,), jnp.float32, smallest / len(split), high / len(split))
        return jnp.repeat(jnp.exp(draws), shape[axis_at] // parts).reshape((-1,) + (1,) * (len(shape) - axis_at - 1))

    factor_of = one(*split[0])
    for cut in split[1:]:
        factor_of = factor_of * one(*cut)
    return factor_of


def routed_block(rng, own, number, rows, amount, top, most, lean):
    sequence = jax.random.permutation(rng, amount)
    packed, usual = load_shares(amount, rows * top, most, lean, True), load_shares(amount, rows * top, most, lean, False)
    places = jnp.arange(amount)

    def named(lengths, offset_by):
        used = int((lengths > 0).sum())
        fixed = max(1, used // 4)
        shifted = fixed + (places - fixed + offset_by * (used - fixed)) % max(1, amount - fixed)
        return jnp.zeros((amount,), jnp.int32).at[sequence[jnp.where(places < fixed, places, shifted)]].set(jnp.asarray(lengths, jnp.int32))

    lengths = jnp.where(number % 4 == 0, named(packed, number // 4), named(usual, number - number // 4 - 1))
    mixed = jax.random.permutation(jax.random.fold_in(own, 3), amount)
    source_of, receiver = mixed[0:amount // 2 * 2:2], mixed[1:amount // 2 * 2:2]
    room = jnp.minimum(lengths[source_of] - 1, most - lengths[receiver]) // 2
    room = jnp.where((source_of == sequence[0]) | (receiver == sequence[0]) | (lengths[receiver] == 0), 0, jnp.maximum(room, 0))
    shifted = jax.random.randint(jax.random.fold_in(own, 4), (amount // 2,), 0, 1 << 20) % (room + 1)
    lengths = lengths.at[source_of].add(-shifted).at[receiver].add(shifted)
    items = jnp.searchsorted(jnp.cumsum(lengths), jnp.arange(rows * top), side="right").astype(jnp.int32)
    grid = items.reshape(top, rows).T
    grid = grid[jax.random.permutation(jax.random.fold_in(own, 1), rows)]
    offset_by = jax.random.randint(jax.random.fold_in(own, 2), (rows, 1), 0, top)
    return jnp.take_along_axis(grid, (jnp.arange(top)[None, :] + offset_by) % top, axis=1)


def load_shares(number_of, total, reach, skew, full):
    weights = [(1 << 20) // math.isqrt(grade ** skew) + 1 for grade in range(1, number_of + 1)]
    largest = reach if full else min(reach, max(-(-total // number_of), total * weights[0] // sum(weights)))
    least = 1 if total - largest >= number_of - 1 else 0
    holding, rest = [largest] + [least] * (number_of - 1), total - largest - least * (number_of - 1)
    while rest > 0:
        free = [i for i in range(1, number_of) if holding[i] < largest] or [i for i in range(1, number_of) if holding[i] < reach]
        mass, remaining = sum([weights[i] for i in free]), rest
        for i in free:
            addition = min(reach - holding[i], max(1, remaining * weights[i] // mass), rest)
            holding[i] = holding[i] + addition
            rest = rest - addition
    return np.array(holding)


def scatter_about(rng, extent, scale, reach, shards=(), held_as=jnp.bfloat16):
    entries = jax.random.normal(rng, extent, jnp.float32) * scale
    if len(shards) > 0:
        entries = block_scale(rng, extent, shards, -0.22, 0.18) * entries
    return jnp.clip(entries, min=-reach, max=reach).astype(held_as)


def heavy_noise(stream_key, extent, deviation, bound, split, heavy, held_as=jnp.bfloat16):
    values = deviation * jax.random.normal(stream_key, extent, jnp.float32)
    if split:
        values = values * block_scale(stream_key, extent, split, -0.22, 0.18)
    return jnp.clip(strengthened(values, jax.random.fold_in(stream_key, 3), *heavy), -bound, bound).astype(held_as)


def setup_inputs(seed: int = 0) -> dict:
    key_list = jax.random.split(jax.random.key(seed), 11)
    grad_parts = heavy_noise(key_list[0], (N_DP, EXPERTS, FF_W, D), 1.0, 6.0, ((0, 4), (3, 32)), (0, 2, 4, 2.0), jnp.float32)
    master = scatter_about(key_list[1], (EXPERTS, FF_W, D), FF_W ** -0.5, 0.21875, ((1, 4), (2, 32)), jnp.float32)
    moment_one = scatter_about(key_list[2], (EXPERTS, FF_W, D), 0.2, 1.2, ((1, 4), (2, 32)), jnp.float32)
    moment_two = jnp.clip(jnp.exp(math.log(0.5) - 2.3025851 * jax.random.uniform(key_list[3], (EXPERTS, FF_W, D), jnp.float32) ** block_scale(key_list[3], (EXPERTS, FF_W, D), ((1, 4), (2, 32)), -0.2, 0.2)), 0.05, 0.5)
    gate_owned = scatter_about(key_list[4], (EXPERTS, FF_W, D), D ** -0.5, 0.09375, ((0, 32), (1, 4)))
    up_owned = scatter_about(key_list[5], (EXPERTS, FF_W, D), D ** -0.5, 0.09375, ((0, 32), (1, 4)))
    tokens = scatter_about(key_list[6], (TOKENS, D), 1.0, 6.0, ((0, 128),))
    expert_ids_keys = jax.random.split(jax.random.fold_in(key_list[7], 1), TOKENS // TOK_DEV)
    expert_ids_turns = jax.random.permutation(jax.random.fold_in(key_list[7], 3), TOKENS // TOK_DEV)
    expert_ids = jax.vmap(lambda own, number: routed_block(jax.random.fold_in(key_list[7], 2), own, number, TOK_DEV, EXPERTS, TOP, CAP, 2))(expert_ids_keys, expert_ids_turns).reshape((TOKENS, TOP))
    gate_values = jnp.clip(jnp.exp(math.log(1.0) - 2.9957323 * jax.random.uniform(key_list[8], (TOKENS, TOP), jnp.float32) ** block_scale(key_list[8], (TOKENS, TOP), ((0, 128),), -0.2, 0.2)), 0.05, 1.0)
    owner_map = jax.random.permutation(key_list[9], EXPERTS).astype(jnp.int32)
    return dict(grad_parts=grad_parts, master=master, moment_one=moment_one, moment_two=moment_two, gate_owned=gate_owned, up_owned=up_owned, tokens=tokens, expert_ids=expert_ids, gate_values=gate_values, owner_map=owner_map)


beta_one = 0.9
beta_two = 0.95
epsilon = 1e-08
learn_rate = 0.02
decay_rate = 0.1
bias_one = 1.0 - 0.9 ** 10
bias_two = 1.0 - 0.95 ** 10

def reference(grad_parts, master, moment_one, moment_two, gate_owned, up_owned, tokens, expert_ids, gate_values, owner_map):
    gradient = lax.optimization_barrier(jnp.sum(grad_parts, axis=0))
    first_mom = beta_one * moment_one + (1.0 - beta_one) * gradient
    second_mom = beta_two * moment_two + (1.0 - beta_two) * gradient * gradient
    step_dir = first_mom / bias_one / (jnp.sqrt(second_mom / bias_two) + epsilon)
    new_master = master - learn_rate * (step_dir + decay_rate * master)
    owned_down = jnp.zeros(new_master.shape, jnp.bfloat16).at[owner_map].set(new_master.astype(jnp.bfloat16))
    block_size = FF_W // N_DP
    flat_ids = expert_ids.reshape(-1)
    token_at = (jnp.arange(TOKENS * TOP) // TOP).astype(jnp.int32)
    gate_flat = gate_values.reshape(-1)
    max_rows = min(TOKENS, N_FSDP * N_DP * CAP)

    def per_expert(carry, expert):
        miss_key = (flat_ids != expert).astype(jnp.int32)
        ordering = jnp.argsort(miss_key, stable=True)[:max_rows]
        is_live = miss_key[ordering] == 0
        chosen = token_at[ordering]
        row_block = tokens[chosen]
        owner_row = owner_map[expert]
        gate_mat = gate_owned[owner_row]
        up_mat = up_owned[owner_row]
        down_mat = owned_down[owner_row]
        dims = (((1,), (1,)), ((), ()))
        gate_pre = lax.dot_general(row_block, gate_mat, dims, preferred_element_type=jnp.float32)
        up_pre = lax.dot_general(row_block, up_mat, dims, preferred_element_type=jnp.float32)
        hidden = (jax.nn.silu(gate_pre) * up_pre).astype(jnp.bfloat16)
        total = jnp.zeros((max_rows, D), jnp.float32)
        for quarter in range(N_DP):
            lower = quarter * block_size
            partial_value = jnp.dot(hidden[:, lower:lower + block_size], down_mat[lower:lower + block_size], preferred_element_type=jnp.float32)
            rounded = lax.optimization_barrier(partial_value.astype(jnp.bfloat16))
            total = total + rounded.astype(jnp.float32)
        expert_out = total.astype(jnp.bfloat16)
        weight = jnp.where(is_live, gate_flat[ordering], jnp.zeros_like(gate_flat[ordering]))
        carry = carry.at[chosen].add(weight[:, None] * expert_out.astype(jnp.float32))
        return (carry, None)
    start = jnp.zeros((TOKENS, D), jnp.float32)
    summed, _ = lax.scan(per_expert, start, jnp.arange(EXPERTS).astype(jnp.int32))
    return (owned_down, summed.astype(jnp.bfloat16))
```

```python
import jax
import jax.numpy as jnp
from jax import lax
from jax.experimental import pallas as pl
from jax.experimental.pallas import tpu as pltpu
from jax.sharding import PartitionSpec as P

MESH = pl.DeviceIdType.MESH

beta_one = 0.9
beta_two = 0.95
epsilon = 1e-08
learn_rate = 0.02
decay_rate = 0.1
bias_one = 1.0 - 0.9**10
bias_two = 1.0 - 0.95**10

NY, NX, NC, NZ = 4, 4, 2, 4
NF = NY * NX * NC
EXPERTS = 32
ROWS = 192
HALF = ROWS // 2
COLS = 128
D = 4096
TOK = 8
CAP = 4
TOKENS = 1024
EXTRA = 128
WIDE = D // 2 + EXTRA
TCOLS = 2 * WIDE
BLK = 256
NBLK = TOKENS // BLK
SLOTS = BLK // TOK * CAP
CHUNKS = 8
PER = EXPERTS // CHUNKS

OFFSETS = (
    ((2, 2), (1, 0)),
    ((2, 1), (1, 2)),
    ((2, 3), (3, 2)),
    ((2, 0), (0, 2)),
    ((1, 1), (3, 3)),
    ((1, 3), (3, 1)),
    ((0, 1), (3, 0)),
    ((0, 3), (0, 0)),
)

BF = jnp.bfloat16
F32 = jnp.float32
NT = (((1,), (1,)), ((), ()))
TN = (((0,), (0,)), ((), ()))
NN = (((1,), (0,)), ((), ()))


def dot(a, b, dims):
    return lax.dot_general(a, b, dims, preferred_element_type=F32)


def adam(g, m, m1, m2):
    first = beta_one * m1 + (1.0 - beta_one) * g
    second = beta_two * m2 + (1.0 - beta_two) * g * g
    step = (first / bias_one) / (jnp.sqrt(second / bias_two) + epsilon)
    return m - learn_rate * (step + decay_rate * m)


def kernel(
    inv, pay, grads, master, mom1, mom2, gate, up,
    owned, combined,
    gb0, gb1, gb2, gb3, st, gu, zb, tok, hb, pos, wrow,
    hs, hr, ds_, dr, fs, fr, wn, acc, zf, zs, zr, zsum, comb,
    lsem, hsem, dsem, fsem, wsem, psem, tsem, asem, zsem, csem,
):
    f = lax.axis_index("fsdp")
    z = lax.axis_index("dp")
    y, x, c = f // 8, lax.rem(f // 2, 4), lax.rem(f, 2)

    def m4(v):
        return lax.rem(v + 4, 4)

    def fid(yy, xx, cc):
        return (yy * 4 + xx) * 2 + cc

    pending = []

    def send(src, dst, sem, i, dev):
        cp = pltpu.make_async_remote_copy(
            src_ref=src, dst_ref=dst, send_sem=sem.at[0, i], recv_sem=sem.at[1, i],
            device_id=dev, device_id_type=MESH,
        )
        cp.start()
        pending.append(cp)

    def arrived(dst, sem, i):
        pltpu.make_async_remote_copy(
            src_ref=dst, dst_ref=dst, send_sem=sem.at[0, i], recv_sem=sem.at[1, i],
            device_id=(f, m4(z + 1)), device_id_type=MESH,
        ).wait_recv()

    gb = (gb0, gb1, gb2, gb3)
    quarter = (m4(z + 2), m4(z + 1), m4(z - 1), z)

    def load_g(k):
        return pltpu.make_async_copy(grads.at[0, :, pl.ds(quarter[k] * ROWS, ROWS), :], gb[k], lsem.at[k])

    loads = [load_g(k) for k in range(4)]
    loads += [pltpu.make_async_copy(r, st.at[k], lsem.at[4 + k]) for k, r in enumerate((master, mom1, mom2))]
    loads += [pltpu.make_async_copy(r.at[0], gu.at[pl.ds(k * ROWS, ROWS)], lsem.at[7 + k]) for k, r in enumerate((gate, up))]
    for cp in loads:
        cp.start()

    barrier = pltpu.get_barrier_semaphore()

    def greet(p, carry):
        pl.semaphore_signal(barrier, inc=1, device_id=(lax.rem(f + p, NF), z), device_id_type=MESH)
        return carry

    lax.fori_loop(1, NF, greet, 0)
    for k in range(1, NZ):
        pl.semaphore_signal(barrier, inc=1, device_id=(f, m4(z + k)), device_id_type=MESH)
    pl.semaphore_wait(barrier, NF - 1 + NZ - 1)

    for k in (2, 1, 3):
        send(pay, zb.at[z], psem, k, (f, m4(z + k)))
    zb[z] = pay[...]

    def owner(j, i):
        dx, dy = OFFSETS[j][i // 2]
        return m4(y + dy), m4(x + dx), lax.rem(c + i % 2, 2)

    def expert(j, i):
        return inv[fid(*owner(j, i))]

    up_z, down_z = (f, m4(z + 1)), (f, m4(z - 1))
    low, high = pl.ds(0, HALF), pl.ds(HALF, HALF)

    def step_h(j):
        for i in range(PER):
            e = expert(j, i)
            hs[0, j, i] = gb[0][e, low, :].astype(BF)
            hs[1, j, i] = gb[0][e, high, :].astype(BF)
        send(hs.at[0, j], hr.at[0, j], hsem, j, up_z)
        send(hs.at[1, j], hr.at[1, j], hsem, CHUNKS + j, down_z)

    def step_d(j):
        for i in range(PER):
            e = expert(j, i)
            ds_[0, j, i] = gb[1][e, high, :].astype(BF)
            ds_[1, j, i] = gb[2][e, low, :].astype(BF)
        send(ds_.at[0, j], dr.at[0, j], dsem, j, up_z)
        send(ds_.at[1, j], dr.at[1, j], dsem, CHUNKS + j, down_z)

    def step_f(j):
        arrived(hr.at[0, j], hsem, j)
        arrived(hr.at[1, j], hsem, CHUNKS + j)
        for i in range(PER):
            e = expert(j, i)
            fs[0, j, i] = (gb[1][e, low, :] + hr[0, j, i].astype(F32)).astype(BF)
            fs[1, j, i] = (gb[2][e, high, :] + hr[1, j, i].astype(F32)).astype(BF)
        send(fs.at[0, j], fr.at[0, j], fsem, j, up_z)
        send(fs.at[1, j], fr.at[1, j], fsem, CHUNKS + j, down_z)

    def step_n(j):
        for k in range(2):
            arrived(fr.at[k, j], fsem, k * CHUNKS + j)
            arrived(dr.at[k, j], dsem, k * CHUNKS + j)
        for i in range(PER):
            e = expert(j, i)
            p = j * PER + i

            def tile(t, carry, e=e, p=p, i=i):
                r = pl.multiple_of(t * 16, 16)
                for k in range(2):
                    rows = pl.ds(k * HALF + r, 16)
                    g = gb[3][e, rows, :] + fr[k, j, i, pl.ds(r, 16), :].astype(F32)
                    g = g + dr[1 - k, j, i, pl.ds(r, 16), :].astype(F32)
                    new = adam(g, st[0, e, rows, :], st[1, e, rows, :], st[2, e, rows, :])
                    wn[p, rows, :] = new.astype(BF)
                return carry

            lax.fori_loop(0, HALF // 16, tile, 0)
            mine = pl.ds(pl.multiple_of(f * COLS, COLS), COLS)
            oy, ox, oc = owner(j, i)
            if OFFSETS[j][i // 2] == (0, 0) and i % 2 == 0:
                cp = pltpu.make_async_copy(wn.at[p], owned.at[0, :, mine], lsem.at[9])
                cp.start()
                own_copy.append(cp)
            else:
                send(wn.at[p], owned.at[0, :, mine], wsem, p, (fid(oy, ox, oc), z))

    own_copy = []

    def gather(buf, sem):
        n_rows, n_cols = buf.shape[-2:]
        halves = (pl.ds(0, n_rows // 2), pl.ds(n_rows // 2, n_rows // 2))
        whole = pl.ds(0, n_cols)
        parts = (pl.ds(0, n_cols // 2), pl.ds(n_cols // 2, n_cols // 2))
        own = ((y, x), (x, y))

        def ref(h, p, s, cols):
            if h == 0:
                return buf.at[p, s, c, halves[0], cols]
            return buf.at[s, p, c, halves[1], cols]

        def dev(h, p, s):
            return (fid(p, s, c), z) if h == 0 else (fid(s, p, c), z)

        def go(h, p, s, cols, i, to):
            r = ref(h, p, s, cols)
            send(r, r, sem, h * 20 + i, dev(h, *to))

        order = (0, -1, 1, 2)

        def secondary(h, k):
            p, s = own[h]
            i = 4 + 4 * order.index(k)
            go(h, m4(p + k), s, whole, i, (p, m4(s + 1)))
            go(h, m4(p + k), s, whole, i + 1, (p, m4(s - 1)))

        def forward(h, k):
            p, s = own[h]
            i = 4 + 4 * order.index(k)
            q = m4(p + k)
            arrived(ref(h, q, m4(s - 1), whole), sem, h * 20 + i)
            go(h, q, m4(s - 1), parts[0], i + 2, (p, m4(s + 1)))
            arrived(ref(h, q, m4(s + 1), whole), sem, h * 20 + i + 1)
            go(h, q, m4(s + 1), parts[1], i + 3, (p, m4(s - 1)))

        for h in (0, 1):
            p, s = own[h]
            go(h, p, s, whole, 0, (m4(p + 1), s))
            go(h, p, s, whole, 1, (m4(p - 1), s))
        for h in (0, 1):
            secondary(h, 0)
        yield
        for h in (0, 1):
            p, s = own[h]
            arrived(ref(h, m4(p - 1), s, whole), sem, h * 20)
            go(h, m4(p - 1), s, parts[0], 2, (m4(p + 1), s))
            secondary(h, -1)
            arrived(ref(h, m4(p + 1), s, whole), sem, h * 20 + 1)
            go(h, m4(p + 1), s, parts[1], 3, (m4(p - 1), s))
            secondary(h, 1)
        yield
        for h in (0, 1):
            forward(h, 0)
        yield
        for h in (0, 1):
            p, s = own[h]
            arrived(ref(h, m4(p + 2), s, parts[0]), sem, h * 20 + 2)
            arrived(ref(h, m4(p + 2), s, parts[1]), sem, h * 20 + 3)
            secondary(h, 2)
        yield
        for h in (0, 1):
            forward(h, -1)
            forward(h, 1)
        yield
        for h in (0, 1):
            forward(h, 2)
        yield
        for h in (0, 1):
            p, s = own[h]
            for k in order:
                i = h * 20 + 4 + 4 * order.index(k)
                arrived(ref(h, m4(p + k), m4(s + 2), parts[0]), sem, i + 2)
                arrived(ref(h, m4(p + k), m4(s + 2), parts[1]), sem, i + 3)
        mine = buf.at[:, :, c]
        send(mine, mine, sem, 40, (fid(y, x, 1 - c), z))
        yield
        arrived(buf.at[:, :, 1 - c], sem, 40)
        yield

    def pack_tokens():
        for k in (1, 3, 2):
            arrived(zb.at[m4(z - k)], psem, k)
        blocks = [zb[k].astype(F32) for k in range(NZ)]
        first = jnp.concatenate([b[0:TOK] for b in blocks], axis=0).astype(BF)
        last = jnp.concatenate([b[TOK : 2 * TOK] for b in blocks], axis=0).astype(BF)
        half = D // 2
        tok[y, x, c, :, 0:half] = first[:, 0:half]
        tok[y, x, c, :, half:D] = last[:, 0:half]
        tok[y, x, c, :, D : D + EXTRA] = first[:, half:WIDE]
        tok[y, x, c, :, D + EXTRA : TCOLS] = last[:, half:WIDE]

    def hidden():
        row = lax.broadcasted_iota(jnp.int32, (EXPERTS, EXTRA), 0)
        lane = lax.broadcasted_iota(jnp.int32, (EXPERTS, EXTRA), 1)
        eye = (row == lane).astype(F32).astype(BF)
        t_row = lax.broadcasted_iota(jnp.int32, (BLK, BLK), 0)
        t_col = lax.broadcasted_iota(jnp.int32, (BLK, BLK), 1)
        before = ((t_row // TOK == t_col // TOK) & (t_row < t_col)).astype(F32).astype(BF)
        base = (lax.broadcasted_iota(jnp.int32, (EXPERTS, BLK), 1) // TOK * CAP).astype(F32)

        def step(b, carry):
            w_hi = dot(eye, tok[b, :, :, :, D : D + EXTRA].reshape(BLK, EXTRA), NT)
            w_lo = dot(eye, tok[b, :, :, :, D + EXTRA : TCOLS].reshape(BLK, EXTRA), NT)
            routed = w_hi > 0.0
            rank = dot(jnp.where(routed, 1.0, 0.0).astype(BF), before, NN)
            pos[b] = jnp.where(routed, rank + base, -1.0)
            wrow[...] = w_hi + w_lo
            pre = dot(gu[...], tok[b, :, :, :, 0:D].reshape(BLK, D), NT)
            g, u = pre[0:ROWS], pre[ROWS : 2 * ROWS]
            h = g / (1.0 + jnp.exp(-g)) * u * wrow[pl.ds(f, 1), :]
            h = dot(h.astype(BF), select(b, f), NT)
            hb[y, x, c, :, pl.ds(pl.multiple_of(b * SLOTS, SLOTS), SLOTS)] = h.astype(BF)
            return carry

        lax.fori_loop(0, NBLK, step, 0)

    def select(b, o):
        slot = lax.broadcasted_iota(jnp.int32, (SLOTS, BLK), 0).astype(F32)
        return jnp.where(slot == pos[b, pl.ds(o, 1), :], 1.0, 0.0).astype(BF)

    def multiply(j, q):
        parts = []
        for i in (2 * q, 2 * q + 1):
            oy, ox, oc = owner(j, i)
            parts.append(dot(wn[j * PER + i], hb[oy, ox, oc], TN).astype(BF))
        for b in range(NBLK):
            cut = slice(b * SLOTS, (b + 1) * SLOTS)
            both = jnp.concatenate([part[:, cut] for part in parts], axis=1)
            sel = jnp.concatenate([select(b, fid(*owner(j, i))) for i in (2 * q, 2 * q + 1)], axis=0)
            acc[:, b * BLK : (b + 1) * BLK] += dot(both, sel, NN)

    loads[0].wait()
    for j in range(CHUNKS):
        step_h(j)
    pack_tokens()
    tokens = gather(tok, tsem)
    next(tokens)
    loads[1].wait()
    loads[2].wait()
    step_d(0)
    step_f(0)
    step_d(1)
    next(tokens)
    step_f(1)
    step_d(2)
    next(tokens)
    step_f(2)
    step_d(3)
    for k in range(3, 9):
        loads[k].wait()
    next(tokens)
    step_n(0)
    step_f(3)
    step_d(4)
    next(tokens)
    step_n(1)
    step_f(4)
    step_d(5)
    next(tokens)
    step_n(2)
    step_f(5)
    step_d(6)
    next(tokens)
    step_f(6)
    step_d(7)
    step_f(7)
    next(tokens)
    hidden()
    hids = gather(hb, asem)
    next(hids)
    step_n(3)
    next(hids)
    step_n(4)
    next(hids)
    step_n(5)
    next(hids)
    step_n(6)
    next(hids)
    step_n(7)
    next(hids)
    next(hids)
    acc[...] = jnp.zeros_like(acc)
    next(hids)
    for j in range(CHUNKS):
        for q in range(2):
            multiply(j, q)

    for b in range(NBLK):
        a = acc[:, b * BLK : (b + 1) * BLK].T.reshape(BLK // (NZ * TOK), NZ, TOK, COLS)
        n = BLK // NZ
        for k in range(NZ):
            part = a[:, k].reshape(n, COLS)
            zf[k, b * n : (b + 1) * n, :] = part
            zs[k, b * n : (b + 1) * n, :] = part.astype(BF)
    for k in (2, 1, 3):
        send(zs.at[m4(z + k)], zr.at[k - 1], zsem, k, (f, m4(z + k)))
    total = zf[z]
    for k in (1, 3, 2):
        arrived(zr.at[k - 1], zsem, k)
        total = total + zr[k - 1].astype(F32)
    zsum[...] = total

    def out_copy(p, to):
        return pltpu.make_async_remote_copy(
            src_ref=zsum.at[pl.ds(pl.multiple_of(to * TOK, TOK), TOK)], dst_ref=comb.at[f],
            send_sem=csem.at[0, p], recv_sem=csem.at[1, p], device_id=(to, z), device_id_type=MESH,
        )

    def out_send(p, carry):
        out_copy(p, lax.rem(f + p, NF)).start()
        return carry

    lax.fori_loop(1, NF, out_send, 0)
    comb[f] = zsum[pl.ds(pl.multiple_of(f * TOK, TOK), TOK), :]

    def out_wait(p, carry):
        src = lax.rem(f - p + NF, NF)
        pltpu.make_async_remote_copy(
            src_ref=comb.at[src], dst_ref=comb.at[src], send_sem=csem.at[0, p], recv_sem=csem.at[1, p],
            device_id=(lax.rem(f + p, NF), z), device_id_type=MESH,
        ).wait_recv()
        out_copy(p, lax.rem(f + p, NF)).wait_send()
        return carry

    lax.fori_loop(1, NF, out_wait, 0)
    for k in range(NF):
        combined[:, k * COLS : (k + 1) * COLS] = comb[k].astype(BF)

    for j in range(CHUNKS):
        for i in range(PER):
            dx, dy = OFFSETS[j][i // 2]
            if (dx, dy) == (0, 0) and i % 2 == 0:
                continue
            src = fid(m4(y - dy), m4(x - dx), lax.rem(c + i % 2, 2))
            arrived(owned.at[0, :, pl.ds(pl.multiple_of(src * COLS, COLS), COLS)], wsem, j * PER + i)
    for cp in own_copy:
        cp.wait()
    for cp in pending:
        cp.wait_send()


def local(grad_parts, master, moment_one, moment_two, gate_owned, up_owned, tokens, expert_ids, gate_values, owner_map):
    index = jnp.arange(EXPERTS, dtype=jnp.int32)
    inverse = jnp.sum(jnp.where(owner_map[None, :] == index[:, None], index[None, :], 0), axis=1)
    weight = jnp.sum(
        jnp.where(expert_ids[:, :, None] == inverse[None, None, :], gate_values[:, :, None], 0.0), axis=1
    )
    w_hi = lax.reduce_precision(weight, 8, 7)
    w_lo = lax.reduce_precision(weight - w_hi, 8, 7)
    extra = jnp.concatenate([w_hi, w_lo], axis=0).astype(BF)
    extra = jnp.pad(extra, ((0, 0), (0, EXTRA - EXPERTS)))
    half = D // 2
    pay = jnp.concatenate([jnp.concatenate([tokens[:, :half], tokens[:, half:]], axis=0), extra], axis=1)
    vmem = pl.BlockSpec(memory_space=pltpu.VMEM)
    hbm = pl.BlockSpec(memory_space=pl.ANY)
    dma = pltpu.SemaphoreType.DMA
    ring = (2, CHUNKS, PER, HALF, COLS)
    return pl.pallas_call(
        kernel,
        out_shape=(
            jax.ShapeDtypeStruct((1, ROWS, D), BF),
            jax.ShapeDtypeStruct((TOK, D), BF),
        ),
        in_specs=[pl.BlockSpec(memory_space=pltpu.SMEM), vmem] + [hbm] * 6,
        out_specs=(hbm, vmem),
        scratch_shapes=[
            pltpu.VMEM((EXPERTS, ROWS, COLS), F32),
            pltpu.VMEM((EXPERTS, ROWS, COLS), F32),
            pltpu.VMEM((EXPERTS, ROWS, COLS), F32),
            pltpu.VMEM((EXPERTS, ROWS, COLS), F32),
            pltpu.VMEM((3, EXPERTS, ROWS, COLS), F32),
            pltpu.VMEM((2 * ROWS, D), BF),
            pltpu.VMEM((NZ, 2 * TOK, WIDE), BF),
            pltpu.VMEM((NY, NX, NC, NZ * TOK, TCOLS), BF),
            pltpu.VMEM((NY, NX, NC, ROWS, NBLK * SLOTS), BF),
            pltpu.VMEM((NBLK, EXPERTS, BLK), F32),
            pltpu.VMEM((EXPERTS, BLK), F32),
            pltpu.VMEM(ring, BF),
            pltpu.VMEM(ring, BF),
            pltpu.VMEM(ring, BF),
            pltpu.VMEM(ring, BF),
            pltpu.VMEM(ring, BF),
            pltpu.VMEM(ring, BF),
            pltpu.VMEM((EXPERTS, ROWS, COLS), BF),
            pltpu.VMEM((COLS, TOKENS), F32),
            pltpu.VMEM((NZ, TOKENS // NZ, COLS), F32),
            pltpu.VMEM((NZ, TOKENS // NZ, COLS), BF),
            pltpu.VMEM((NZ - 1, TOKENS // NZ, COLS), BF),
            pltpu.VMEM((TOKENS // NZ, COLS), F32),
            pltpu.VMEM((NF, TOK, COLS), F32),
            dma((10,)),
            dma((2, 2 * CHUNKS)),
            dma((2, 2 * CHUNKS)),
            dma((2, 2 * CHUNKS)),
            dma((2, EXPERTS)),
            dma((2, NZ)),
            dma((2, 41)),
            dma((2, 41)),
            dma((2, NZ)),
            dma((2, NF)),
        ],
        compiler_params=pltpu.CompilerParams(
            collective_id=0, has_side_effects=True, vmem_limit_bytes=60 * 2**20
        ),
    )(inverse, pay, grad_parts, master, moment_one, moment_two, gate_owned, up_owned)


def solution(mesh):
    in_specs = (
        P("dp", None, None, "fsdp"),
        P(None, "dp", "fsdp"),
        P(None, "dp", "fsdp"),
        P(None, "dp", "fsdp"),
        P("fsdp", "dp", None),
        P("fsdp", "dp", None),
        P(("fsdp", "dp"), None),
        P(("fsdp", "dp"), None),
        P(("fsdp", "dp"), None),
        P(),
    )
    out_specs = (P("fsdp", "dp", None), P(("fsdp", "dp"), None))
    return jax.shard_map(local, mesh=mesh, in_specs=in_specs, out_specs=out_specs, check_vma=False)
```

```python
import jax
import jax.numpy as jnp
from jax import lax
from jax.experimental import pallas as pl
from jax.experimental.pallas import tpu as pltpu
from jax.sharding import PartitionSpec as P

MESH = pl.DeviceIdType.MESH

beta_one = 0.9
beta_two = 0.95
epsilon = 1e-08
learn_rate = 0.02
decay_rate = 0.1
bias_one = 1.0 - 0.9**10
bias_two = 1.0 - 0.95**10

NY, NX, NC, NZ = 4, 4, 2, 4
NF = NY * NX * NC
EXPERTS = 32
ROWS = 192
HALF = ROWS // 2
COLS = 128
D = 4096
TOK = 8
CAP = 4
TOKENS = 1024
EXTRA = 128
WIDE = D // 2 + EXTRA
TCOLS = 2 * WIDE
BLK = 256
NBLK = TOKENS // BLK
SLOTS = BLK // TOK * CAP
CHUNKS = 8
PER = EXPERTS // CHUNKS

OFFSETS = (
    ((2, 2), (1, 0)),
    ((2, 1), (1, 2)),
    ((2, 3), (3, 2)),
    ((2, 0), (0, 2)),
    ((1, 1), (3, 3)),
    ((1, 3), (3, 1)),
    ((0, 1), (3, 0)),
    ((0, 3), (0, 0)),
)

BF = jnp.bfloat16
F32 = jnp.float32
NT = (((1,), (1,)), ((), ()))
TN = (((0,), (0,)), ((), ()))
NN = (((1,), (0,)), ((), ()))


def dot(a, b, dims):
    return lax.dot_general(a, b, dims, preferred_element_type=F32)


def adam(g, m, m1, m2):
    first = beta_one * m1 + (1.0 - beta_one) * g
    second = beta_two * m2 + (1.0 - beta_two) * g * g
    step = (first / bias_one) / (jnp.sqrt(second / bias_two) + epsilon)
    return m - learn_rate * (step + decay_rate * m)


def kernel(
    omap, tokens, ids, gates, grads, master, mom1, mom2, gate, up,
    owned, combined,
    inv, gb0, gb1, gb2, gb3, st, gu, pay, zb, tok, hb, pos, wrow,
    hs, hr, ds_, dr, fs, fr, wn, acc, zf, zs, zr, zsum, comb,
    lsem, hsem, dsem, fsem, wsem, psem, tsem, asem, zsem, csem,
):
    f = lax.axis_index("fsdp")
    z = lax.axis_index("dp")
    y, x, c = f // 8, lax.rem(f // 2, 4), lax.rem(f, 2)

    def m4(v):
        return lax.rem(v + 4, 4)

    def fid(yy, xx, cc):
        return (yy * 4 + xx) * 2 + cc

    pending = []

    def send(src, dst, sem, i, dev):
        cp = pltpu.make_async_remote_copy(
            src_ref=src, dst_ref=dst, send_sem=sem.at[0, i], recv_sem=sem.at[1, i],
            device_id=dev, device_id_type=MESH,
        )
        cp.start()
        pending.append(cp)

    def arrived(dst, sem, i):
        pltpu.make_async_remote_copy(
            src_ref=dst, dst_ref=dst, send_sem=sem.at[0, i], recv_sem=sem.at[1, i],
            device_id=(f, m4(z + 1)), device_id_type=MESH,
        ).wait_recv()

    gb = (gb0, gb1, gb2, gb3)
    quarter = (m4(z + 2), m4(z + 1), m4(z - 1), z)

    def load_g(k):
        return pltpu.make_async_copy(grads.at[0, :, pl.ds(quarter[k] * ROWS, ROWS), :], gb[k], lsem.at[k])

    loads = [load_g(k) for k in range(4)]
    loads += [pltpu.make_async_copy(r, st.at[k], lsem.at[4 + k]) for k, r in enumerate((master, mom1, mom2))]
    loads += [pltpu.make_async_copy(r.at[0], gu.at[pl.ds(k * ROWS, ROWS)], lsem.at[7 + k]) for k, r in enumerate((gate, up))]
    for cp in loads[0:3]:
        cp.start()

    barrier = pltpu.get_barrier_semaphore()

    for near in (fid(y, x, 1 - c), fid(y, m4(x + 1), c), fid(y, m4(x - 1), c), fid(m4(y + 1), x, c), fid(m4(y - 1), x, c)):
        pl.semaphore_signal(barrier, inc=1, device_id=(near, z), device_id_type=MESH)
    for k in range(1, NZ):
        pl.semaphore_signal(barrier, inc=1, device_id=(f, m4(z + k)), device_id_type=MESH)

    lane = lax.broadcasted_iota(jnp.int32, (TOK, EXTRA), 1)
    invrow = jnp.full((TOK, EXTRA), -1, jnp.int32)
    for e in range(EXPERTS):
        invrow = jnp.where(lane == omap[e], e, invrow)
    weight = jnp.zeros((TOK, EXTRA), F32)
    for k in range(TOK):
        weight += jnp.where(ids[:, k : k + 1] == invrow, gates[:, k : k + 1], 0.0)
    w_hi = weight.astype(BF).astype(F32)
    half_d = D // 2
    rows = tokens[...].astype(F32)
    pay[:, 0:half_d] = jnp.concatenate([rows[:, 0:half_d], rows[:, half_d:D]], axis=0).astype(BF)
    pay[:, half_d:WIDE] = jnp.concatenate([w_hi, weight - w_hi], axis=0).astype(BF)

    def invert(o, carry):
        found = 0
        for e in range(EXPERTS):
            found = jnp.where(omap[e] == o, e, found)
        inv[o] = found
        return carry

    lax.fori_loop(0, EXPERTS, invert, 0)
    pl.semaphore_wait(barrier, NZ - 1 + 5)

    for k in (2, 1, 3):
        send(pay, zb.at[z], psem, k, (f, m4(z + k)))
    zb[z] = pay[...]

    def owner(j, i):
        dx, dy = OFFSETS[j][i // 2]
        return m4(y + dy), m4(x + dx), lax.rem(c + i % 2, 2)

    def expert(j, i):
        return inv[fid(*owner(j, i))]

    def place(j, i):
        dx, dy = OFFSETS[j][i // 2]
        return (dy * 4 + dx) * 2 + i % 2

    up_z, down_z = (f, m4(z + 1)), (f, m4(z - 1))
    low, high = pl.ds(0, HALF), pl.ds(HALF, HALF)

    def step_h(j):
        for i in range(PER):
            e = expert(j, i)
            hs[0, j, i] = gb[0][e, low, :].astype(BF)
            hs[1, j, i] = gb[0][e, high, :].astype(BF)
        send(hs.at[0, j], hr.at[0, j], hsem, j, up_z)
        send(hs.at[1, j], hr.at[1, j], hsem, CHUNKS + j, down_z)

    def step_d(j):
        for i in range(PER):
            e = expert(j, i)
            ds_[0, j, i] = gb[1][e, high, :].astype(BF)
            ds_[1, j, i] = gb[2][e, low, :].astype(BF)
        send(ds_.at[0, j], dr.at[0, j], dsem, j, up_z)
        send(ds_.at[1, j], dr.at[1, j], dsem, CHUNKS + j, down_z)

    def step_f(j):
        arrived(hr.at[0, j], hsem, j)
        arrived(hr.at[1, j], hsem, CHUNKS + j)
        for i in range(PER):
            e = expert(j, i)
            fs[0, j, i] = (gb[1][e, low, :] + hr[0, j, i].astype(F32)).astype(BF)
            fs[1, j, i] = (gb[2][e, high, :] + hr[1, j, i].astype(F32)).astype(BF)
        send(fs.at[0, j], fr.at[0, j], fsem, j, up_z)
        send(fs.at[1, j], fr.at[1, j], fsem, CHUNKS + j, down_z)

    def step_n(j):
        for k in range(2):
            arrived(fr.at[k, j], fsem, k * CHUNKS + j)
            arrived(dr.at[k, j], dsem, k * CHUNKS + j)
        for i in range(PER):
            e = expert(j, i)
            p = place(j, i)

            def tile(t, carry, e=e, p=p, i=i):
                r = pl.multiple_of(t * 16, 16)
                for k in range(2):
                    rows = pl.ds(k * HALF + r, 16)
                    g = gb[3][e, rows, :] + fr[k, j, i, pl.ds(r, 16), :].astype(F32)
                    g = g + dr[1 - k, j, i, pl.ds(r, 16), :].astype(F32)
                    new = adam(g, st[0, e, rows, :], st[1, e, rows, :], st[2, e, rows, :])
                    wn[p, rows, :] = new.astype(BF)
                return carry

            lax.fori_loop(0, HALF // 16, tile, 0)

    def step_w(j):
        mine = pl.ds(pl.multiple_of(f * COLS, COLS), COLS)
        for i in range(PER):
            p = place(j, i)
            if p == 0:
                cp = pltpu.make_async_copy(wn.at[p], owned.at[0, :, mine], lsem.at[9])
                cp.start()
                own_copy.append(cp)
            else:
                send(wn.at[p], owned.at[0, :, mine], wsem, p, (fid(*owner(j, i)), z))

    own_copy = []

    def gather(buf, sem):
        n_rows, n_cols = buf.shape[-2:]
        halves = (pl.ds(0, n_rows // 2), pl.ds(n_rows // 2, n_rows // 2))
        whole = pl.ds(0, n_cols)
        parts = (pl.ds(0, n_cols // 2), pl.ds(n_cols // 2, n_cols // 2))
        own = ((y, x), (x, y))

        def ref(h, p, s, cols):
            if h == 0:
                return buf.at[p, s, c, halves[0], cols]
            return buf.at[s, p, c, halves[1], cols]

        def dev(h, p, s):
            return (fid(p, s, c), z) if h == 0 else (fid(s, p, c), z)

        def go(h, p, s, cols, i, to):
            r = ref(h, p, s, cols)
            send(r, r, sem, h * 20 + i, dev(h, *to))

        order = (0, -1, 1, 2)

        def secondary(h, k):
            p, s = own[h]
            i = 4 + 4 * order.index(k)
            go(h, m4(p + k), s, whole, i, (p, m4(s + 1)))
            go(h, m4(p + k), s, whole, i + 1, (p, m4(s - 1)))

        def forward(h, k):
            p, s = own[h]
            i = 4 + 4 * order.index(k)
            q = m4(p + k)
            arrived(ref(h, q, m4(s - 1), whole), sem, h * 20 + i)
            go(h, q, m4(s - 1), parts[0], i + 2, (p, m4(s + 1)))
            arrived(ref(h, q, m4(s + 1), whole), sem, h * 20 + i + 1)
            go(h, q, m4(s + 1), parts[1], i + 3, (p, m4(s - 1)))

        sent = []

        def share(h, p, s):
            i = 40 + len(sent)
            r = ref(h, p, s, whole)
            send(r, r, sem, i, (fid(y, x, 1 - c), z))
            other = buf.at[p, s, 1 - c, halves[0]] if h == 0 else buf.at[s, p, 1 - c, halves[1]]
            sent.append((other, i))

        def shared(first, last):
            for other, i in sent[first:last]:
                arrived(other, sem, i)

        for h in (0, 1):
            p, s = own[h]
            go(h, p, s, whole, 0, (m4(p + 1), s))
            go(h, p, s, whole, 1, (m4(p - 1), s))
        for h in (0, 1):
            secondary(h, 0)
            share(h, *own[h])
        yield
        for h in (0, 1):
            p, s = own[h]
            arrived(ref(h, m4(p - 1), s, whole), sem, h * 20)
            go(h, m4(p - 1), s, parts[0], 2, (m4(p + 1), s))
            secondary(h, -1)
            arrived(ref(h, m4(p + 1), s, whole), sem, h * 20 + 1)
            go(h, m4(p + 1), s, parts[1], 3, (m4(p - 1), s))
            secondary(h, 1)
        yield
        for h in (0, 1):
            p, s = own[h]
            forward(h, 0)
            for k in (-1, 1):
                share(h, m4(p + k), s)
                share(h, p, m4(s + k))
        yield
        for h in (0, 1):
            p, s = own[h]
            arrived(ref(h, m4(p + 2), s, parts[0]), sem, h * 20 + 2)
            arrived(ref(h, m4(p + 2), s, parts[1]), sem, h * 20 + 3)
            secondary(h, 2)
        yield
        for h in (0, 1):
            p, s = own[h]
            for k in (-1, 1):
                forward(h, k)
                share(h, m4(p + k), m4(s - 1))
                share(h, m4(p + k), m4(s + 1))
        near = len(sent)
        yield
        for h in (0, 1):
            p, s = own[h]
            share(h, m4(p + 2), s)
            forward(h, 2)
            share(h, m4(p + 2), m4(s - 1))
            share(h, m4(p + 2), m4(s + 1))
        shared(0, near)
        yield
        far = len(sent)
        for h in (0, 1):
            p, s = own[h]
            for k in order:
                i = h * 20 + 4 + 4 * order.index(k)
                arrived(ref(h, m4(p + k), m4(s + 2), parts[0]), sem, i + 2)
                arrived(ref(h, m4(p + k), m4(s + 2), parts[1]), sem, i + 3)
                share(h, m4(p + k), m4(s + 2))
        shared(near, far)
        shared(far, len(sent))
        yield

    def pack_tokens():
        for k in (1, 3, 2):
            arrived(zb.at[m4(z - k)], psem, k)
        blocks = [zb[k].astype(F32) for k in range(NZ)]
        first = jnp.concatenate([b[0:TOK] for b in blocks], axis=0).astype(BF)
        last = jnp.concatenate([b[TOK : 2 * TOK] for b in blocks], axis=0).astype(BF)
        half = D // 2
        tok[y, x, c, :, 0:half] = first[:, 0:half]
        tok[y, x, c, :, half:D] = last[:, 0:half]
        tok[y, x, c, :, D : D + EXTRA] = first[:, half:WIDE]
        tok[y, x, c, :, D + EXTRA : TCOLS] = last[:, half:WIDE]

    def hidden():
        row = lax.broadcasted_iota(jnp.int32, (EXPERTS, EXTRA), 0)
        lane = lax.broadcasted_iota(jnp.int32, (EXPERTS, EXTRA), 1)
        eye = (row == lane).astype(F32).astype(BF)
        t_row = lax.broadcasted_iota(jnp.int32, (BLK, BLK), 0)
        t_col = lax.broadcasted_iota(jnp.int32, (BLK, BLK), 1)
        before = ((t_row // TOK == t_col // TOK) & (t_row < t_col)).astype(F32).astype(BF)
        base = (lax.broadcasted_iota(jnp.int32, (EXPERTS, BLK), 1) // TOK * CAP).astype(F32)

        def step(b, carry):
            w_hi = dot(eye, tok[b, :, :, :, D : D + EXTRA].reshape(BLK, EXTRA), NT)
            w_lo = dot(eye, tok[b, :, :, :, D + EXTRA : TCOLS].reshape(BLK, EXTRA), NT)
            routed = w_hi > 0.0
            rank = dot(jnp.where(routed, 1.0, 0.0).astype(BF), before, NN)
            pos[b] = jnp.where(routed, rank + base, -1.0)
            wrow[...] = w_hi + w_lo
            pre = dot(gu[...], tok[b, :, :, :, 0:D].reshape(BLK, D), NT)
            g, u = pre[0:ROWS], pre[ROWS : 2 * ROWS]
            h = g / (1.0 + jnp.exp(-g)) * u * wrow[pl.ds(f, 1), :]
            h = dot(h.astype(BF), select(b, f), NT)
            hb[y, x, c, :, pl.ds(pl.multiple_of(b * SLOTS, SLOTS), SLOTS)] = h.astype(BF)
            return carry

        lax.fori_loop(0, NBLK, step, 0)

    def select(b, o):
        slot = lax.broadcasted_iota(jnp.int32, (SLOTS, BLK), 0).astype(F32)
        return jnp.where(slot == pos[b, pl.ds(o, 1), :], 1.0, 0.0).astype(BF)

    def multiply(dx, dy):
        oy, ox = m4(y + dy), m4(x + dx)
        parts, owners = [], []
        for dc in range(NC):
            oc = lax.rem(c + dc, 2)
            owners.append(fid(oy, ox, oc))
            parts.append(dot(wn[(dy * 4 + dx) * 2 + dc], hb[oy, ox, oc], TN).astype(BF))
        for b in range(NBLK):
            cut = slice(b * SLOTS, (b + 1) * SLOTS)
            both = jnp.concatenate([part[:, cut] for part in parts], axis=1)
            sel = jnp.concatenate([select(b, o) for o in owners], axis=0)
            acc[:, b * BLK : (b + 1) * BLK] += dot(both, sel, NN)

    def skip(d):
        return d + d // 2

    def multiply_near(n, carry):
        multiply(skip(n % 3), skip(n // 3))
        return carry

    def multiply_row(n, carry):
        multiply(n, 2)
        return carry

    def multiply_column(n, carry):
        multiply(2, skip(n))
        return carry

    loads[0].wait()
    for j in range(CHUNKS):
        step_h(j)
    pack_tokens()
    tokens_all = gather(tok, tsem)
    next(tokens_all)
    for k in range(3, 9):
        loads[k].start()
    loads[1].wait()
    loads[2].wait()
    step_d(0)
    step_d(1)
    step_f(0)
    next(tokens_all)
    step_f(1)
    step_d(2)
    next(tokens_all)
    step_f(2)
    step_d(3)
    next(tokens_all)
    for k in range(3, 9):
        loads[k].wait()
    step_f(3)
    step_d(4)
    step_f(4)
    step_d(5)
    next(tokens_all)
    step_f(5)
    step_d(6)
    step_n(0)
    next(tokens_all)
    step_f(6)
    step_d(7)
    step_f(7)
    next(tokens_all)
    step_w(0)
    hidden()
    hids = gather(hb, asem)
    next(hids)
    step_n(1)
    next(hids)
    step_n(2)
    next(hids)
    step_n(3)
    next(hids)
    step_n(4)
    next(hids)
    step_w(1)
    step_w(2)
    step_n(5)
    next(hids)
    step_w(3)
    step_w(4)
    step_w(5)
    step_n(6)
    step_w(6)
    step_n(7)
    step_w(7)
    acc[...] = jnp.zeros_like(acc)
    lax.fori_loop(0, 9, multiply_near, 0)
    next(hids)
    lax.fori_loop(0, 4, multiply_row, 0)
    lax.fori_loop(0, 3, multiply_column, 0)

    for b in range(NBLK):
        a = acc[:, b * BLK : (b + 1) * BLK].T.reshape(BLK // (NZ * TOK), NZ, TOK, COLS)
        n = BLK // NZ
        for k in range(NZ):
            part = a[:, k].reshape(n, COLS)
            zf[k, b * n : (b + 1) * n, :] = part
            zs[k, b * n : (b + 1) * n, :] = part.astype(BF)
    for k in (2, 1, 3):
        send(zs.at[m4(z + k)], zr.at[k - 1], zsem, k, (f, m4(z + k)))
    total = zf[z]
    for k in (1, 3, 2):
        arrived(zr.at[k - 1], zsem, k)
        total = total + zr[k - 1].astype(F32)
    zsum[...] = total

    def out_copy(p, to):
        return pltpu.make_async_remote_copy(
            src_ref=zsum.at[pl.ds(pl.multiple_of(to * TOK, TOK), TOK)], dst_ref=comb.at[f],
            send_sem=csem.at[0, p], recv_sem=csem.at[1, p], device_id=(to, z), device_id_type=MESH,
        )

    def out_send(p, carry):
        out_copy(p, lax.rem(f + p, NF)).start()
        return carry

    lax.fori_loop(1, NF, out_send, 0)
    comb[f] = zsum[pl.ds(pl.multiple_of(f * TOK, TOK), TOK), :]

    def out_wait(p, carry):
        src = lax.rem(f - p + NF, NF)
        pltpu.make_async_remote_copy(
            src_ref=comb.at[src], dst_ref=comb.at[src], send_sem=csem.at[0, p], recv_sem=csem.at[1, p],
            device_id=(lax.rem(f + p, NF), z), device_id_type=MESH,
        ).wait_recv()
        out_copy(p, lax.rem(f + p, NF)).wait_send()
        return carry

    lax.fori_loop(1, NF, out_wait, 0)
    for k in range(NF):
        combined[:, k * COLS : (k + 1) * COLS] = comb[k].astype(BF)

    for j in range(CHUNKS):
        for i in range(PER):
            dx, dy = OFFSETS[j][i // 2]
            if (dx, dy) == (0, 0) and i % 2 == 0:
                continue
            src = fid(m4(y - dy), m4(x - dx), lax.rem(c + i % 2, 2))
            arrived(owned.at[0, :, pl.ds(pl.multiple_of(src * COLS, COLS), COLS)], wsem, place(j, i))
    for cp in own_copy:
        cp.wait()
    for cp in pending:
        cp.wait_send()


def local(grad_parts, master, moment_one, moment_two, gate_owned, up_owned, tokens, expert_ids, gate_values, owner_map):
    vmem = pl.BlockSpec(memory_space=pltpu.VMEM)
    hbm = pl.BlockSpec(memory_space=pl.ANY)
    dma = pltpu.SemaphoreType.DMA
    ring = (2, CHUNKS, PER, HALF, COLS)
    return pl.pallas_call(
        kernel,
        out_shape=(
            jax.ShapeDtypeStruct((1, ROWS, D), BF),
            jax.ShapeDtypeStruct((TOK, D), BF),
        ),
        in_specs=[pl.BlockSpec(memory_space=pltpu.SMEM)] + [vmem] * 3 + [hbm] * 6,
        out_specs=(hbm, vmem),
        scratch_shapes=[
            pltpu.SMEM((EXPERTS,), jnp.int32),
            pltpu.VMEM((EXPERTS, ROWS, COLS), F32),
            pltpu.VMEM((EXPERTS, ROWS, COLS), F32),
            pltpu.VMEM((EXPERTS, ROWS, COLS), F32),
            pltpu.VMEM((EXPERTS, ROWS, COLS), F32),
            pltpu.VMEM((3, EXPERTS, ROWS, COLS), F32),
            pltpu.VMEM((2 * ROWS, D), BF),
            pltpu.VMEM((2 * TOK, WIDE), BF),
            pltpu.VMEM((NZ, 2 * TOK, WIDE), BF),
            pltpu.VMEM((NY, NX, NC, NZ * TOK, TCOLS), BF),
            pltpu.VMEM((NY, NX, NC, ROWS, NBLK * SLOTS), BF),
            pltpu.VMEM((NBLK, EXPERTS, BLK), F32),
            pltpu.VMEM((EXPERTS, BLK), F32),
            pltpu.VMEM(ring, BF),
            pltpu.VMEM(ring, BF),
            pltpu.VMEM(ring, BF),
            pltpu.VMEM(ring, BF),
            pltpu.VMEM(ring, BF),
            pltpu.VMEM(ring, BF),
            pltpu.VMEM((EXPERTS, ROWS, COLS), BF),
            pltpu.VMEM((COLS, TOKENS), F32),
            pltpu.VMEM((NZ, TOKENS // NZ, COLS), F32),
            pltpu.VMEM((NZ, TOKENS // NZ, COLS), BF),
            pltpu.VMEM((NZ - 1, TOKENS // NZ, COLS), BF),
            pltpu.VMEM((TOKENS // NZ, COLS), F32),
            pltpu.VMEM((NF, TOK, COLS), F32),
            dma((10,)),
            dma((2, 2 * CHUNKS)),
            dma((2, 2 * CHUNKS)),
            dma((2, 2 * CHUNKS)),
            dma((2, EXPERTS)),
            dma((2, NZ)),
            dma((2, 72)),
            dma((2, 72)),
            dma((2, NZ)),
            dma((2, NF)),
        ],
        compiler_params=pltpu.CompilerParams(
            collective_id=0, has_side_effects=True, vmem_limit_bytes=60 * 2**20
        ),
    )(owner_map, tokens, expert_ids, gate_values, grad_parts, master, moment_one, moment_two, gate_owned, up_owned)


def solution(mesh):
    in_specs = (
        P("dp", None, None, "fsdp"),
        P(None, "dp", "fsdp"),
        P(None, "dp", "fsdp"),
        P(None, "dp", "fsdp"),
        P("fsdp", "dp", None),
        P("fsdp", "dp", None),
        P(("fsdp", "dp"), None),
        P(("fsdp", "dp"), None),
        P(("fsdp", "dp"), None),
        P(),
    )
    out_specs = (P("fsdp", "dp", None), P(("fsdp", "dp"), None))
    return jax.shard_map(local, mesh=mesh, in_specs=in_specs, out_specs=out_specs, check_vma=False)
```

```python
import jax
import jax.numpy as jnp
from jax import lax
from jax.experimental import pallas as pl
from jax.experimental.pallas import tpu as pltpu
from jax.sharding import PartitionSpec as P

MESH = pl.DeviceIdType.MESH

beta_one = 0.9
beta_two = 0.95
epsilon = 1e-08
learn_rate = 0.02
decay_rate = 0.1
bias_one = 1.0 - 0.9**10
bias_two = 1.0 - 0.95**10

NY, NX, NC, NZ = 4, 4, 2, 4
NF = NY * NX * NC
EXPERTS = 32
ROWS = 192
HALF = ROWS // 2
COLS = 128
D = 4096
TOK = 8
CAP = 4
TOKENS = 1024
EXTRA = 128
WIDE = D // 2 + EXTRA
TCOLS = 2 * WIDE
BLK = 256
NBLK = TOKENS // BLK
SLOTS = BLK // TOK * CAP
CHUNKS = 8
PER = EXPERTS // CHUNKS

OFFSETS = (
    ((2, 2), (1, 0)),
    ((2, 1), (1, 2)),
    ((2, 3), (3, 2)),
    ((2, 0), (0, 2)),
    ((1, 1), (3, 3)),
    ((1, 3), (3, 1)),
    ((0, 1), (3, 0)),
    ((0, 3), (0, 0)),
)

BF = jnp.bfloat16
F32 = jnp.float32
NT = (((1,), (1,)), ((), ()))
TN = (((0,), (0,)), ((), ()))
NN = (((1,), (0,)), ((), ()))


def dot(a, b, dims):
    return lax.dot_general(a, b, dims, preferred_element_type=F32)


def adam(g, m, m1, m2):
    first = beta_one * m1 + (1.0 - beta_one) * g
    second = beta_two * m2 + (1.0 - beta_two) * g * g
    step = (first / bias_one) / (jnp.sqrt(second / bias_two) + epsilon)
    return m - learn_rate * (step + decay_rate * m)


def kernel(
    omap, tokens, ids, gates, grads, master, mom1, mom2, gate, up,
    owned, combined,
    inv, gb0, gb1, gb2, gb3, st, gu, pay, zb, tok, hb, pos, wrow,
    hs, hr, ds_, dr, fs, fr, wn, acc, zf, zs, zr, zsum, comb,
    lsem, hsem, dsem, fsem, wsem, psem, tsem, asem, zsem, csem,
):
    f = lax.axis_index("fsdp")
    z = lax.axis_index("dp")
    y, x, c = f // 8, lax.rem(f // 2, 4), lax.rem(f, 2)

    def m4(v):
        return lax.rem(v + 4, 4)

    def fid(yy, xx, cc):
        return (yy * 4 + xx) * 2 + cc

    pending = []

    def send(src, dst, sem, i, dev):
        cp = pltpu.make_async_remote_copy(
            src_ref=src, dst_ref=dst, send_sem=sem.at[0, i], recv_sem=sem.at[1, i],
            device_id=dev, device_id_type=MESH,
        )
        cp.start()
        pending.append(cp)

    def arrived(dst, sem, i):
        pltpu.make_async_remote_copy(
            src_ref=dst, dst_ref=dst, send_sem=sem.at[0, i], recv_sem=sem.at[1, i],
            device_id=(f, m4(z + 1)), device_id_type=MESH,
        ).wait_recv()

    gb = (gb0, gb1, gb2, gb3)
    quarter = (m4(z + 2), m4(z + 1), m4(z - 1), z)

    def load_g(k):
        return pltpu.make_async_copy(grads.at[0, :, pl.ds(quarter[k] * ROWS, ROWS), :], gb[k], lsem.at[k])

    loads = [load_g(k) for k in range(4)]
    loads += [pltpu.make_async_copy(r, st.at[k], lsem.at[4 + k]) for k, r in enumerate((master, mom1, mom2))]
    loads += [pltpu.make_async_copy(r.at[0], gu.at[pl.ds(k * ROWS, ROWS)], lsem.at[7 + k]) for k, r in enumerate((gate, up))]
    for cp in loads[0:3]:
        cp.start()

    barrier = pltpu.get_barrier_semaphore()

    for near in (fid(y, x, 1 - c), fid(y, m4(x + 1), c), fid(y, m4(x - 1), c), fid(m4(y + 1), x, c), fid(m4(y - 1), x, c)):
        pl.semaphore_signal(barrier, inc=1, device_id=(near, z), device_id_type=MESH)
    for k in range(1, NZ):
        pl.semaphore_signal(barrier, inc=1, device_id=(f, m4(z + k)), device_id_type=MESH)

    lane = lax.broadcasted_iota(jnp.int32, (TOK, EXTRA), 1)
    invrow = jnp.full((TOK, EXTRA), -1, jnp.int32)
    for e in range(EXPERTS):
        invrow = jnp.where(lane == omap[e], e, invrow)
    weight = jnp.zeros((TOK, EXTRA), F32)
    for k in range(TOK):
        weight += jnp.where(ids[:, k : k + 1] == invrow, gates[:, k : k + 1], 0.0)
    w_hi = weight.astype(BF).astype(F32)
    half_d = D // 2
    rows = tokens[...].astype(F32)
    pay[:, 0:half_d] = jnp.concatenate([rows[:, 0:half_d], rows[:, half_d:D]], axis=0).astype(BF)
    pay[:, half_d:WIDE] = jnp.concatenate([w_hi, weight - w_hi], axis=0).astype(BF)

    def invert(o, carry):
        found = 0
        for e in range(EXPERTS):
            found = jnp.where(omap[e] == o, e, found)
        inv[o] = found
        return carry

    lax.fori_loop(0, EXPERTS, invert, 0)
    pl.semaphore_wait(barrier, NZ - 1 + 5)

    for k in (2, 1, 3):
        send(pay, zb.at[z], psem, k, (f, m4(z + k)))
    zb[z] = pay[...]

    def owner(j, i):
        dx, dy = OFFSETS[j][i // 2]
        return m4(y + dy), m4(x + dx), lax.rem(c + i % 2, 2)

    def expert(j, i):
        return inv[fid(*owner(j, i))]

    def place(j, i):
        dx, dy = OFFSETS[j][i // 2]
        return (dy * 4 + dx) * 2 + i % 2

    up_z, down_z = (f, m4(z + 1)), (f, m4(z - 1))
    low, high = pl.ds(0, HALF), pl.ds(HALF, HALF)

    def step_h(j):
        for i in range(PER):
            e = expert(j, i)
            hs[0, j, i] = gb[0][e, low, :].astype(BF)
            hs[1, j, i] = gb[0][e, high, :].astype(BF)
        send(hs.at[0, j], hr.at[0, j], hsem, j, up_z)
        send(hs.at[1, j], hr.at[1, j], hsem, CHUNKS + j, down_z)

    def step_d(j):
        for i in range(PER):
            e = expert(j, i)
            ds_[0, j, i] = gb[1][e, high, :].astype(BF)
            ds_[1, j, i] = gb[2][e, low, :].astype(BF)
        send(ds_.at[0, j], dr.at[0, j], dsem, j, up_z)
        send(ds_.at[1, j], dr.at[1, j], dsem, CHUNKS + j, down_z)

    def step_f(j):
        arrived(hr.at[0, j], hsem, j)
        arrived(hr.at[1, j], hsem, CHUNKS + j)
        for i in range(PER):
            e = expert(j, i)
            fs[0, j, i] = (gb[1][e, low, :] + hr[0, j, i].astype(F32)).astype(BF)
            fs[1, j, i] = (gb[2][e, high, :] + hr[1, j, i].astype(F32)).astype(BF)
        send(fs.at[0, j], fr.at[0, j], fsem, j, up_z)
        send(fs.at[1, j], fr.at[1, j], fsem, CHUNKS + j, down_z)

    def step_n(j):
        for k in range(2):
            arrived(fr.at[k, j], fsem, k * CHUNKS + j)
            arrived(dr.at[k, j], dsem, k * CHUNKS + j)
        for i in range(PER):
            e = expert(j, i)
            p = place(j, i)

            def tile(t, carry, e=e, p=p, i=i):
                r = pl.multiple_of(t * 16, 16)
                for k in range(2):
                    rows = pl.ds(k * HALF + r, 16)
                    g = gb[3][e, rows, :] + fr[k, j, i, pl.ds(r, 16), :].astype(F32)
                    g = g + dr[1 - k, j, i, pl.ds(r, 16), :].astype(F32)
                    new = adam(g, st[0, e, rows, :], st[1, e, rows, :], st[2, e, rows, :])
                    wn[p, rows, :] = new.astype(BF)
                return carry

            lax.fori_loop(0, HALF // 16, tile, 0)

    def step_w(j):
        mine = pl.ds(pl.multiple_of(f * COLS, COLS), COLS)
        for i in range(PER):
            p = place(j, i)
            if p == 0:
                cp = pltpu.make_async_copy(wn.at[p], owned.at[0, :, mine], lsem.at[9])
                cp.start()
                own_copy.append(cp)
            else:
                send(wn.at[p], owned.at[0, :, mine], wsem, p, (fid(*owner(j, i)), z))

    own_copy = []

    def gather(buf, sem):
        n_rows, n_cols = buf.shape[-2:]
        halves = (pl.ds(0, n_rows // 2), pl.ds(n_rows // 2, n_rows // 2))
        whole = pl.ds(0, n_cols)
        parts = (pl.ds(0, n_cols // 2), pl.ds(n_cols // 2, n_cols // 2))
        own = ((y, x), (x, y))

        def ref(h, p, s, cols):
            if h == 0:
                return buf.at[p, s, c, halves[0], cols]
            return buf.at[s, p, c, halves[1], cols]

        def dev(h, p, s):
            return (fid(p, s, c), z) if h == 0 else (fid(s, p, c), z)

        def go(h, p, s, cols, i, to):
            r = ref(h, p, s, cols)
            send(r, r, sem, h * 20 + i, dev(h, *to))

        order = (0, -1, 1, 2)

        def secondary(h, k):
            p, s = own[h]
            i = 4 + 4 * order.index(k)
            go(h, m4(p + k), s, whole, i, (p, m4(s + 1)))
            go(h, m4(p + k), s, whole, i + 1, (p, m4(s - 1)))

        def forward(h, k):
            p, s = own[h]
            i = 4 + 4 * order.index(k)
            q = m4(p + k)
            arrived(ref(h, q, m4(s - 1), whole), sem, h * 20 + i)
            go(h, q, m4(s - 1), parts[0], i + 2, (p, m4(s + 1)))
            arrived(ref(h, q, m4(s + 1), whole), sem, h * 20 + i + 1)
            go(h, q, m4(s + 1), parts[1], i + 3, (p, m4(s - 1)))

        sent = []

        def share(h, p, s):
            i = 40 + len(sent)
            r = ref(h, p, s, whole)
            send(r, r, sem, i, (fid(y, x, 1 - c), z))
            other = buf.at[p, s, 1 - c, halves[0]] if h == 0 else buf.at[s, p, 1 - c, halves[1]]
            sent.append((other, i))

        def shared(first, last):
            for other, i in sent[first:last]:
                arrived(other, sem, i)

        for h in (0, 1):
            p, s = own[h]
            go(h, p, s, whole, 0, (m4(p + 1), s))
            go(h, p, s, whole, 1, (m4(p - 1), s))
        for h in (0, 1):
            secondary(h, 0)
            share(h, *own[h])
        yield
        for h in (0, 1):
            p, s = own[h]
            arrived(ref(h, m4(p - 1), s, whole), sem, h * 20)
            go(h, m4(p - 1), s, parts[0], 2, (m4(p + 1), s))
            secondary(h, -1)
            arrived(ref(h, m4(p + 1), s, whole), sem, h * 20 + 1)
            go(h, m4(p + 1), s, parts[1], 3, (m4(p - 1), s))
            secondary(h, 1)
        yield
        for h in (0, 1):
            p, s = own[h]
            forward(h, 0)
            for k in (-1, 1):
                share(h, m4(p + k), s)
                share(h, p, m4(s + k))
        yield
        for h in (0, 1):
            p, s = own[h]
            arrived(ref(h, m4(p + 2), s, parts[0]), sem, h * 20 + 2)
            arrived(ref(h, m4(p + 2), s, parts[1]), sem, h * 20 + 3)
            secondary(h, 2)
        yield
        for h in (0, 1):
            p, s = own[h]
            for k in (-1, 1):
                forward(h, k)
                share(h, m4(p + k), m4(s - 1))
                share(h, m4(p + k), m4(s + 1))
        near = len(sent)
        yield
        for h in (0, 1):
            p, s = own[h]
            share(h, m4(p + 2), s)
            forward(h, 2)
            share(h, m4(p + 2), m4(s - 1))
            share(h, m4(p + 2), m4(s + 1))
        shared(0, near)
        yield
        far = len(sent)
        for h in (0, 1):
            p, s = own[h]
            for k in order:
                i = h * 20 + 4 + 4 * order.index(k)
                arrived(ref(h, m4(p + k), m4(s + 2), parts[0]), sem, i + 2)
                arrived(ref(h, m4(p + k), m4(s + 2), parts[1]), sem, i + 3)
                share(h, m4(p + k), m4(s + 2))
        shared(near, far)
        shared(far, len(sent))
        yield

    def pack_tokens():
        for k in (1, 3, 2):
            arrived(zb.at[m4(z - k)], psem, k)
        blocks = [zb[k].astype(F32) for k in range(NZ)]
        first = jnp.concatenate([b[0:TOK] for b in blocks], axis=0).astype(BF)
        last = jnp.concatenate([b[TOK : 2 * TOK] for b in blocks], axis=0).astype(BF)
        half = D // 2
        tok[y, x, c, :, 0:half] = first[:, 0:half]
        tok[y, x, c, :, half:D] = last[:, 0:half]
        tok[y, x, c, :, D : D + EXTRA] = first[:, half:WIDE]
        tok[y, x, c, :, D + EXTRA : TCOLS] = last[:, half:WIDE]

    def hidden():
        row = lax.broadcasted_iota(jnp.int32, (EXPERTS, EXTRA), 0)
        lane = lax.broadcasted_iota(jnp.int32, (EXPERTS, EXTRA), 1)
        eye = (row == lane).astype(F32).astype(BF)
        t_row = lax.broadcasted_iota(jnp.int32, (BLK, BLK), 0)
        t_col = lax.broadcasted_iota(jnp.int32, (BLK, BLK), 1)
        before = ((t_row // TOK == t_col // TOK) & (t_row < t_col)).astype(F32).astype(BF)
        base = (lax.broadcasted_iota(jnp.int32, (EXPERTS, BLK), 1) // TOK * CAP).astype(F32)

        def step(b, carry):
            w_hi = dot(eye, tok[b, :, :, :, D : D + EXTRA].reshape(BLK, EXTRA), NT)
            w_lo = dot(eye, tok[b, :, :, :, D + EXTRA : TCOLS].reshape(BLK, EXTRA), NT)
            routed = w_hi > 0.0
            rank = dot(jnp.where(routed, 1.0, 0.0).astype(BF), before, NN)
            pos[b] = jnp.where(routed, rank + base, -1.0)
            wrow[...] = w_hi + w_lo
            pre = dot(gu[...], tok[b, :, :, :, 0:D].reshape(BLK, D), NT)
            g, u = pre[0:ROWS], pre[ROWS : 2 * ROWS]
            h = g / (1.0 + jnp.exp(-g)) * u * wrow[pl.ds(f, 1), :]
            h = dot(h.astype(BF), select(b, f), NT)
            hb[y, x, c, :, pl.ds(pl.multiple_of(b * SLOTS, SLOTS), SLOTS)] = h.astype(BF)
            return carry

        lax.fori_loop(0, NBLK, step, 0)

    def select(b, o):
        slot = lax.broadcasted_iota(jnp.int32, (SLOTS, BLK), 0).astype(F32)
        return jnp.where(slot == pos[b, pl.ds(o, 1), :], 1.0, 0.0).astype(BF)

    def multiply(dx, dy):
        oy, ox = m4(y + dy), m4(x + dx)
        parts, owners = [], []
        for dc in range(NC):
            oc = lax.rem(c + dc, 2)
            owners.append(fid(oy, ox, oc))
            parts.append(dot(wn[(dy * 4 + dx) * 2 + dc], hb[oy, ox, oc], TN).astype(BF))
        for b in range(NBLK):
            cut = slice(b * SLOTS, (b + 1) * SLOTS)
            both = jnp.concatenate([part[:, cut] for part in parts], axis=1)
            sel = jnp.concatenate([select(b, o) for o in owners], axis=0)
            acc[:, b * BLK : (b + 1) * BLK] += dot(both, sel, NN)

    def skip(d):
        return d + d // 2

    def multiply_near(n, carry):
        multiply(skip(n % 3), skip(n // 3))
        return carry

    def multiply_row(n, carry):
        multiply(n, 2)
        return carry

    def multiply_column(n, carry):
        multiply(2, skip(n))
        return carry

    for k in range(3, 9):
        loads[k].start()
    loads[0].wait()
    for j in range(CHUNKS):
        step_h(j)
    pack_tokens()
    tokens_all = gather(tok, tsem)
    next(tokens_all)
    loads[1].wait()
    loads[2].wait()
    step_d(0)
    step_d(1)
    step_f(0)
    next(tokens_all)
    step_f(1)
    step_d(2)
    next(tokens_all)
    step_f(2)
    step_d(3)
    next(tokens_all)
    step_f(3)
    step_d(4)
    step_f(4)
    step_d(5)
    next(tokens_all)
    step_f(5)
    step_d(6)
    for k in range(3, 9):
        loads[k].wait()
    step_n(0)
    next(tokens_all)
    step_f(6)
    step_d(7)
    step_f(7)
    next(tokens_all)
    hidden()
    hids = gather(hb, asem)
    next(hids)
    step_n(1)
    next(hids)
    step_n(2)
    next(hids)
    step_n(3)
    next(hids)
    step_n(4)
    next(hids)
    step_n(5)
    next(hids)
    step_w(0)
    step_w(1)
    step_n(6)
    step_n(7)
    acc[...] = jnp.zeros_like(acc)
    lax.fori_loop(0, 9, multiply_near, 0, unroll=3)
    step_w(2)
    step_w(3)
    step_w(4)
    step_w(5)
    next(hids)
    step_w(6)
    step_w(7)
    lax.fori_loop(0, 4, multiply_row, 0, unroll=2)
    lax.fori_loop(0, 3, multiply_column, 0, unroll=3)

    for b in range(NBLK):
        a = acc[:, b * BLK : (b + 1) * BLK].T.reshape(BLK // (NZ * TOK), NZ, TOK, COLS)
        n = BLK // NZ
        for k in range(NZ):
            part = a[:, k].reshape(n, COLS)
            zf[k, b * n : (b + 1) * n, :] = part
            zs[k, b * n : (b + 1) * n, :] = part.astype(BF)
    for k in (2, 1, 3):
        send(zs.at[m4(z + k)], zr.at[k - 1], zsem, k, (f, m4(z + k)))
    total = zf[z]
    for k in (1, 3, 2):
        arrived(zr.at[k - 1], zsem, k)
        total = total + zr[k - 1].astype(F32)
    zsum[...] = total

    def out_copy(p, to):
        return pltpu.make_async_remote_copy(
            src_ref=zsum.at[pl.ds(pl.multiple_of(to * TOK, TOK), TOK)], dst_ref=comb.at[f],
            send_sem=csem.at[0, p], recv_sem=csem.at[1, p], device_id=(to, z), device_id_type=MESH,
        )

    def out_send(p, carry):
        out_copy(p, lax.rem(f + p, NF)).start()
        return carry

    lax.fori_loop(1, NF, out_send, 0)
    comb[f] = zsum[pl.ds(pl.multiple_of(f * TOK, TOK), TOK), :]

    def out_wait(p, carry):
        src = lax.rem(f - p + NF, NF)
        pltpu.make_async_remote_copy(
            src_ref=comb.at[src], dst_ref=comb.at[src], send_sem=csem.at[0, p], recv_sem=csem.at[1, p],
            device_id=(lax.rem(f + p, NF), z), device_id_type=MESH,
        ).wait_recv()
        out_copy(p, lax.rem(f + p, NF)).wait_send()
        return carry

    lax.fori_loop(1, NF, out_wait, 0)
    for k in range(NF):
        combined[:, k * COLS : (k + 1) * COLS] = comb[k].astype(BF)

    for j in range(CHUNKS):
        for i in range(PER):
            dx, dy = OFFSETS[j][i // 2]
            if (dx, dy) == (0, 0) and i % 2 == 0:
                continue
            src = fid(m4(y - dy), m4(x - dx), lax.rem(c + i % 2, 2))
            arrived(owned.at[0, :, pl.ds(pl.multiple_of(src * COLS, COLS), COLS)], wsem, place(j, i))
    for cp in own_copy:
        cp.wait()
    for cp in pending:
        cp.wait_send()


def local(grad_parts, master, moment_one, moment_two, gate_owned, up_owned, tokens, expert_ids, gate_values, owner_map):
    vmem = pl.BlockSpec(memory_space=pltpu.VMEM)
    hbm = pl.BlockSpec(memory_space=pl.ANY)
    dma = pltpu.SemaphoreType.DMA
    ring = (2, CHUNKS, PER, HALF, COLS)
    return pl.pallas_call(
        kernel,
        out_shape=(
            jax.ShapeDtypeStruct((1, ROWS, D), BF),
            jax.ShapeDtypeStruct((TOK, D), BF),
        ),
        in_specs=[pl.BlockSpec(memory_space=pltpu.SMEM)] + [vmem] * 3 + [hbm] * 6,
        out_specs=(hbm, vmem),
        scratch_shapes=[
            pltpu.SMEM((EXPERTS,), jnp.int32),
            pltpu.VMEM((EXPERTS, ROWS, COLS), F32),
            pltpu.VMEM((EXPERTS, ROWS, COLS), F32),
            pltpu.VMEM((EXPERTS, ROWS, COLS), F32),
            pltpu.VMEM((EXPERTS, ROWS, COLS), F32),
            pltpu.VMEM((3, EXPERTS, ROWS, COLS), F32),
            pltpu.VMEM((2 * ROWS, D), BF),
            pltpu.VMEM((2 * TOK, WIDE), BF),
            pltpu.VMEM((NZ, 2 * TOK, WIDE), BF),
            pltpu.VMEM((NY, NX, NC, NZ * TOK, TCOLS), BF),
            pltpu.VMEM((NY, NX, NC, ROWS, NBLK * SLOTS), BF),
            pltpu.VMEM((NBLK, EXPERTS, BLK), F32),
            pltpu.VMEM((EXPERTS, BLK), F32),
            pltpu.VMEM(ring, BF),
            pltpu.VMEM(ring, BF),
            pltpu.VMEM(ring, BF),
            pltpu.VMEM(ring, BF),
            pltpu.VMEM(ring, BF),
            pltpu.VMEM(ring, BF),
            pltpu.VMEM((EXPERTS, ROWS, COLS), BF),
            pltpu.VMEM((COLS, TOKENS), F32),
            pltpu.VMEM((NZ, TOKENS // NZ, COLS), F32),
            pltpu.VMEM((NZ, TOKENS // NZ, COLS), BF),
            pltpu.VMEM((NZ - 1, TOKENS // NZ, COLS), BF),
            pltpu.VMEM((TOKENS // NZ, COLS), F32),
            pltpu.VMEM((NF, TOK, COLS), F32),
            dma((10,)),
            dma((2, 2 * CHUNKS)),
            dma((2, 2 * CHUNKS)),
            dma((2, 2 * CHUNKS)),
            dma((2, EXPERTS)),
            dma((2, NZ)),
            dma((2, 72)),
            dma((2, 72)),
            dma((2, NZ)),
            dma((2, NF)),
        ],
        compiler_params=pltpu.CompilerParams(
            collective_id=0, has_side_effects=True, vmem_limit_bytes=60 * 2**20
        ),
    )(owner_map, tokens, expert_ids, gate_values, grad_parts, master, moment_one, moment_two, gate_owned, up_owned)


def solution(mesh):
    in_specs = (
        P("dp", None, None, "fsdp"),
        P(None, "dp", "fsdp"),
        P(None, "dp", "fsdp"),
        P(None, "dp", "fsdp"),
        P("fsdp", "dp", None),
        P("fsdp", "dp", None),
        P(("fsdp", "dp"), None),
        P(("fsdp", "dp"), None),
        P(("fsdp", "dp"), None),
        P(),
    )
    out_specs = (P("fsdp", "dp", None), P(("fsdp", "dp"), None))
    return jax.shard_map(local, mesh=mesh, in_specs=in_specs, out_specs=out_specs, check_vma=False)
```

```python
import jax
import jax.numpy as jnp
from jax import lax
from jax.experimental import pallas as pl
from jax.experimental.pallas import tpu as pltpu
from jax.sharding import PartitionSpec as P

MESH = pl.DeviceIdType.MESH

beta_one = 0.9
beta_two = 0.95
epsilon = 1e-08
learn_rate = 0.02
decay_rate = 0.1
bias_one = 1.0 - 0.9**10
bias_two = 1.0 - 0.95**10

NY, NX, NC, NZ = 4, 4, 2, 4
NF = NY * NX * NC
EXPERTS = 32
ROWS = 192
HALF = ROWS // 2
COLS = 128
D = 4096
TOK = 8
CAP = 4
TOKENS = 1024
EXTRA = 128
WIDE = D // 2 + EXTRA
TCOLS = 2 * WIDE
BLK = 256
NBLK = TOKENS // BLK
SLOTS = BLK // TOK * CAP
CHUNKS = 8
PER = EXPERTS // CHUNKS

OFFSETS = (
    ((2, 2), (1, 0)),
    ((2, 1), (1, 2)),
    ((2, 3), (3, 2)),
    ((2, 0), (0, 2)),
    ((1, 1), (3, 3)),
    ((1, 3), (3, 1)),
    ((0, 1), (3, 0)),
    ((0, 3), (0, 0)),
)

BF = jnp.bfloat16
F32 = jnp.float32
NT = (((1,), (1,)), ((), ()))
TN = (((0,), (0,)), ((), ()))
NN = (((1,), (0,)), ((), ()))


def dot(a, b, dims):
    return lax.dot_general(a, b, dims, preferred_element_type=F32)


def adam(g, m, m1, m2):
    first = beta_one * m1 + (1.0 - beta_one) * g
    second = beta_two * m2 + (1.0 - beta_two) * g * g
    step = (first / bias_one) / (jnp.sqrt(second / bias_two) + epsilon)
    return m - learn_rate * (step + decay_rate * m)


def kernel(
    omap, tokens, ids, gates, grads, master, mom1, mom2, gate, up,
    owned, combined,
    inv, gb0, gb1, gb2, gb3, st, gu, pay, zb, tok, hb, pos, wrow,
    hs, hr, ds_, dr, fs, fr, wn, acc, zf, zs, zr, zsum, comb,
    lsem, hsem, dsem, fsem, wsem, psem, tsem, asem, zsem, csem,
):
    f = lax.axis_index("fsdp")
    z = lax.axis_index("dp")
    y, x, c = f // 8, lax.rem(f // 2, 4), lax.rem(f, 2)

    def m4(v):
        return lax.rem(v + 4, 4)

    def fid(yy, xx, cc):
        return (yy * 4 + xx) * 2 + cc

    pending = []

    def send(src, dst, sem, i, dev):
        cp = pltpu.make_async_remote_copy(
            src_ref=src, dst_ref=dst, send_sem=sem.at[0, i], recv_sem=sem.at[1, i],
            device_id=dev, device_id_type=MESH,
        )
        cp.start()
        pending.append(cp)

    def arrived(dst, sem, i):
        pltpu.make_async_remote_copy(
            src_ref=dst, dst_ref=dst, send_sem=sem.at[0, i], recv_sem=sem.at[1, i],
            device_id=(f, m4(z + 1)), device_id_type=MESH,
        ).wait_recv()

    gb = (gb0, gb1, gb2, gb3)
    quarter = (m4(z + 2), m4(z + 1), m4(z - 1), z)

    def load_g(k):
        return pltpu.make_async_copy(grads.at[0, :, pl.ds(quarter[k] * ROWS, ROWS), :], gb[k], lsem.at[k])

    loads = [load_g(k) for k in range(4)]
    loads += [pltpu.make_async_copy(r, st.at[k], lsem.at[4 + k]) for k, r in enumerate((master, mom1, mom2))]
    loads += [pltpu.make_async_copy(r.at[0], gu.at[pl.ds(k * ROWS, ROWS)], lsem.at[7 + k]) for k, r in enumerate((gate, up))]
    for cp in loads[0:3]:
        cp.start()

    barrier = pltpu.get_barrier_semaphore()

    for near in (fid(y, x, 1 - c), fid(y, m4(x + 1), c), fid(y, m4(x - 1), c), fid(m4(y + 1), x, c), fid(m4(y - 1), x, c)):
        pl.semaphore_signal(barrier, inc=1, device_id=(near, z), device_id_type=MESH)
    for k in range(1, NZ):
        pl.semaphore_signal(barrier, inc=1, device_id=(f, m4(z + k)), device_id_type=MESH)

    lane = lax.broadcasted_iota(jnp.int32, (TOK, EXTRA), 1)
    invrow = jnp.full((TOK, EXTRA), -1, jnp.int32)
    for e in range(EXPERTS):
        invrow = jnp.where(lane == omap[e], e, invrow)
    weight = jnp.zeros((TOK, EXTRA), F32)
    for k in range(TOK):
        weight += jnp.where(ids[:, k : k + 1] == invrow, gates[:, k : k + 1], 0.0)
    w_hi = weight.astype(BF).astype(F32)
    half_d = D // 2
    rows = tokens[...].astype(F32)
    pay[:, 0:half_d] = jnp.concatenate([rows[:, 0:half_d], rows[:, half_d:D]], axis=0).astype(BF)
    pay[:, half_d:WIDE] = jnp.concatenate([w_hi, weight - w_hi], axis=0).astype(BF)

    def invert(o, carry):
        found = 0
        for e in range(EXPERTS):
            found = jnp.where(omap[e] == o, e, found)
        inv[o] = found
        return carry

    lax.fori_loop(0, EXPERTS, invert, 0)
    pl.semaphore_wait(barrier, NZ - 1 + 5)

    for k in (2, 1, 3):
        send(pay, zb.at[z], psem, k, (f, m4(z + k)))
    zb[z] = pay[...]

    def owner(j, i):
        dx, dy = OFFSETS[j][i // 2]
        return m4(y + dy), m4(x + dx), lax.rem(c + i % 2, 2)

    def expert(j, i):
        return inv[fid(*owner(j, i))]

    def place(j, i):
        dx, dy = OFFSETS[j][i // 2]
        return (dy * 4 + dx) * 2 + i % 2

    up_z, down_z = (f, m4(z + 1)), (f, m4(z - 1))
    low, high = pl.ds(0, HALF), pl.ds(HALF, HALF)

    def step_h(j):
        for i in range(PER):
            e = expert(j, i)
            hs[0, j, i] = gb[0][e, low, :].astype(BF)
            hs[1, j, i] = gb[0][e, high, :].astype(BF)
        send(hs.at[0, j], hr.at[0, j], hsem, j, up_z)
        send(hs.at[1, j], hr.at[1, j], hsem, CHUNKS + j, down_z)

    def step_d(j):
        for i in range(PER):
            e = expert(j, i)
            ds_[0, j, i] = gb[1][e, high, :].astype(BF)
            ds_[1, j, i] = gb[2][e, low, :].astype(BF)
        send(ds_.at[0, j], dr.at[0, j], dsem, j, up_z)
        send(ds_.at[1, j], dr.at[1, j], dsem, CHUNKS + j, down_z)

    def step_f(j):
        arrived(hr.at[0, j], hsem, j)
        arrived(hr.at[1, j], hsem, CHUNKS + j)
        for i in range(PER):
            e = expert(j, i)
            fs[0, j, i] = (gb[1][e, low, :] + hr[0, j, i].astype(F32)).astype(BF)
            fs[1, j, i] = (gb[2][e, high, :] + hr[1, j, i].astype(F32)).astype(BF)
        send(fs.at[0, j], fr.at[0, j], fsem, j, up_z)
        send(fs.at[1, j], fr.at[1, j], fsem, CHUNKS + j, down_z)

    def step_n(j):
        for k in range(2):
            arrived(fr.at[k, j], fsem, k * CHUNKS + j)
            arrived(dr.at[k, j], dsem, k * CHUNKS + j)
        for i in range(PER):
            e = expert(j, i)
            p = place(j, i)

            def tile(t, carry, e=e, p=p, i=i):
                r = pl.multiple_of(t * 16, 16)
                for k in range(2):
                    rows = pl.ds(k * HALF + r, 16)
                    g = gb[3][e, rows, :] + fr[k, j, i, pl.ds(r, 16), :].astype(F32)
                    g = g + dr[1 - k, j, i, pl.ds(r, 16), :].astype(F32)
                    new = adam(g, st[0, e, rows, :], st[1, e, rows, :], st[2, e, rows, :])
                    wn[p, rows, :] = new.astype(BF)
                return carry

            lax.fori_loop(0, HALF // 16, tile, 0)

    def step_w(j):
        mine = pl.ds(pl.multiple_of(f * COLS, COLS), COLS)
        for i in range(PER):
            p = place(j, i)
            if p == 0:
                cp = pltpu.make_async_copy(wn.at[p], owned.at[0, :, mine], lsem.at[9])
                cp.start()
                own_copy.append(cp)
            else:
                send(wn.at[p], owned.at[0, :, mine], wsem, p, (fid(*owner(j, i)), z))

    own_copy = []

    def gather(buf, sem):
        n_rows, n_cols = buf.shape[-2:]
        halves = (pl.ds(0, n_rows // 2), pl.ds(n_rows // 2, n_rows // 2))
        whole = pl.ds(0, n_cols)
        parts = (pl.ds(0, n_cols // 2), pl.ds(n_cols // 2, n_cols // 2))
        own = ((y, x), (x, y))

        def ref(h, p, s, cols):
            if h == 0:
                return buf.at[p, s, c, halves[0], cols]
            return buf.at[s, p, c, halves[1], cols]

        def dev(h, p, s):
            return (fid(p, s, c), z) if h == 0 else (fid(s, p, c), z)

        def go(h, p, s, cols, i, to):
            r = ref(h, p, s, cols)
            send(r, r, sem, h * 20 + i, dev(h, *to))

        order = (0, -1, 1, 2)

        def secondary(h, k):
            p, s = own[h]
            i = 4 + 4 * order.index(k)
            go(h, m4(p + k), s, whole, i, (p, m4(s + 1)))
            go(h, m4(p + k), s, whole, i + 1, (p, m4(s - 1)))

        def forward(h, k):
            p, s = own[h]
            i = 4 + 4 * order.index(k)
            q = m4(p + k)
            arrived(ref(h, q, m4(s - 1), whole), sem, h * 20 + i)
            go(h, q, m4(s - 1), parts[0], i + 2, (p, m4(s + 1)))
            arrived(ref(h, q, m4(s + 1), whole), sem, h * 20 + i + 1)
            go(h, q, m4(s + 1), parts[1], i + 3, (p, m4(s - 1)))

        sent = []

        def share(h, p, s):
            i = 40 + len(sent)
            r = ref(h, p, s, whole)
            send(r, r, sem, i, (fid(y, x, 1 - c), z))
            other = buf.at[p, s, 1 - c, halves[0]] if h == 0 else buf.at[s, p, 1 - c, halves[1]]
            sent.append((other, i))

        def shared(first, last):
            for other, i in sent[first:last]:
                arrived(other, sem, i)

        for h in (0, 1):
            p, s = own[h]
            go(h, p, s, whole, 0, (m4(p + 1), s))
            go(h, p, s, whole, 1, (m4(p - 1), s))
        for h in (0, 1):
            secondary(h, 0)
            share(h, *own[h])
        yield
        for h in (0, 1):
            p, s = own[h]
            arrived(ref(h, m4(p - 1), s, whole), sem, h * 20)
            go(h, m4(p - 1), s, parts[0], 2, (m4(p + 1), s))
            secondary(h, -1)
            arrived(ref(h, m4(p + 1), s, whole), sem, h * 20 + 1)
            go(h, m4(p + 1), s, parts[1], 3, (m4(p - 1), s))
            secondary(h, 1)
        yield
        for h in (0, 1):
            p, s = own[h]
            forward(h, 0)
            for k in (-1, 1):
                share(h, m4(p + k), s)
                share(h, p, m4(s + k))
        yield
        for h in (0, 1):
            p, s = own[h]
            arrived(ref(h, m4(p + 2), s, parts[0]), sem, h * 20 + 2)
            arrived(ref(h, m4(p + 2), s, parts[1]), sem, h * 20 + 3)
            secondary(h, 2)
        yield
        for h in (0, 1):
            p, s = own[h]
            for k in (-1, 1):
                forward(h, k)
                share(h, m4(p + k), m4(s - 1))
                share(h, m4(p + k), m4(s + 1))
        near = len(sent)
        yield
        for h in (0, 1):
            p, s = own[h]
            share(h, m4(p + 2), s)
            forward(h, 2)
            share(h, m4(p + 2), m4(s - 1))
            share(h, m4(p + 2), m4(s + 1))
        shared(0, near)
        yield
        far = len(sent)
        for h in (0, 1):
            p, s = own[h]
            for k in order:
                i = h * 20 + 4 + 4 * order.index(k)
                arrived(ref(h, m4(p + k), m4(s + 2), parts[0]), sem, i + 2)
                arrived(ref(h, m4(p + k), m4(s + 2), parts[1]), sem, i + 3)
                share(h, m4(p + k), m4(s + 2))
        shared(near, far)
        shared(far, len(sent))
        yield

    def pack_tokens():
        for k in (1, 3, 2):
            arrived(zb.at[m4(z - k)], psem, k)
        blocks = [zb[k].astype(F32) for k in range(NZ)]
        first = jnp.concatenate([b[0:TOK] for b in blocks], axis=0).astype(BF)
        last = jnp.concatenate([b[TOK : 2 * TOK] for b in blocks], axis=0).astype(BF)
        half = D // 2
        tok[y, x, c, :, 0:half] = first[:, 0:half]
        tok[y, x, c, :, half:D] = last[:, 0:half]
        tok[y, x, c, :, D : D + EXTRA] = first[:, half:WIDE]
        tok[y, x, c, :, D + EXTRA : TCOLS] = last[:, half:WIDE]

    def hidden():
        row = lax.broadcasted_iota(jnp.int32, (EXPERTS, EXTRA), 0)
        lane = lax.broadcasted_iota(jnp.int32, (EXPERTS, EXTRA), 1)
        eye = (row == lane).astype(F32).astype(BF)
        t_row = lax.broadcasted_iota(jnp.int32, (BLK, BLK), 0)
        t_col = lax.broadcasted_iota(jnp.int32, (BLK, BLK), 1)
        before = ((t_row // TOK == t_col // TOK) & (t_row < t_col)).astype(F32).astype(BF)
        base = (lax.broadcasted_iota(jnp.int32, (EXPERTS, BLK), 1) // TOK * CAP).astype(F32)

        def step(b, carry):
            w_hi = dot(eye, tok[b, :, :, :, D : D + EXTRA].reshape(BLK, EXTRA), NT)
            w_lo = dot(eye, tok[b, :, :, :, D + EXTRA : TCOLS].reshape(BLK, EXTRA), NT)
            routed = w_hi > 0.0
            rank = dot(jnp.where(routed, 1.0, 0.0).astype(BF), before, NN)
            pos[b] = jnp.where(routed, rank + base, -1.0)
            wrow[...] = w_hi + w_lo
            pre = dot(gu[...], tok[b, :, :, :, 0:D].reshape(BLK, D), NT)
            g, u = pre[0:ROWS], pre[ROWS : 2 * ROWS]
            h = g / (1.0 + jnp.exp(-g)) * u * wrow[pl.ds(f, 1), :]
            h = dot(h.astype(BF), select(b, f), NT)
            hb[y, x, c, :, pl.ds(pl.multiple_of(b * SLOTS, SLOTS), SLOTS)] = h.astype(BF)
            return carry

        lax.fori_loop(0, NBLK, step, 0)

    def select(b, o):
        slot = lax.broadcasted_iota(jnp.int32, (SLOTS, BLK), 0).astype(F32)
        return jnp.where(slot == pos[b, pl.ds(o, 1), :], 1.0, 0.0).astype(BF)

    def multiply(dx, dy):
        oy, ox = m4(y + dy), m4(x + dx)
        parts, owners = [], []
        for dc in range(NC):
            oc = lax.rem(c + dc, 2)
            owners.append(fid(oy, ox, oc))
            parts.append(dot(wn[(dy * 4 + dx) * 2 + dc], hb[oy, ox, oc], TN).astype(BF))
        for b in range(NBLK):
            cut = slice(b * SLOTS, (b + 1) * SLOTS)
            both = jnp.concatenate([part[:, cut] for part in parts], axis=1)
            sel = jnp.concatenate([select(b, o) for o in owners], axis=0)
            acc[:, b * BLK : (b + 1) * BLK] += dot(both, sel, NN)

    def skip(d):
        return d + d // 2

    def multiply_near(n, carry):
        multiply(skip(n % 3), skip(n // 3))
        return carry

    def multiply_row(n, carry):
        multiply(n, 2)
        return carry

    def multiply_column(n, carry):
        multiply(2, skip(n))
        return carry

    for k in range(3, 9):
        loads[k].start()
    loads[0].wait()
    for j in range(CHUNKS):
        step_h(j)
    pack_tokens()
    tokens_all = gather(tok, tsem)
    next(tokens_all)
    loads[1].wait()
    loads[2].wait()
    step_d(0)
    step_d(1)
    step_f(0)
    next(tokens_all)
    step_f(1)
    step_d(2)
    next(tokens_all)
    step_f(2)
    step_d(3)
    next(tokens_all)
    step_f(3)
    step_d(4)
    step_f(4)
    step_d(5)
    next(tokens_all)
    step_f(5)
    step_d(6)
    for k in range(3, 9):
        loads[k].wait()
    step_n(0)
    next(tokens_all)
    step_f(6)
    step_d(7)
    step_f(7)
    next(tokens_all)
    hidden()
    hids = gather(hb, asem)
    next(hids)
    step_n(1)
    next(hids)
    step_n(2)
    next(hids)
    step_n(3)
    next(hids)
    step_n(4)
    next(hids)
    step_n(5)
    next(hids)
    step_n(6)
    step_n(7)
    acc[...] = jnp.zeros_like(acc)
    lax.fori_loop(0, 9, multiply_near, 0, unroll=3)
    step_w(0)
    step_w(1)
    step_w(2)
    step_w(3)
    step_w(4)
    step_w(5)
    next(hids)
    step_w(6)
    step_w(7)
    lax.fori_loop(0, 4, multiply_row, 0, unroll=2)
    lax.fori_loop(0, 3, multiply_column, 0, unroll=3)

    for b in range(NBLK):
        a = acc[:, b * BLK : (b + 1) * BLK].T.reshape(BLK // (NZ * TOK), NZ, TOK, COLS)
        n = BLK // NZ
        for k in range(NZ):
            part = a[:, k].reshape(n, COLS)
            zf[k, b * n : (b + 1) * n, :] = part
            zs[k, b * n : (b + 1) * n, :] = part.astype(BF)
    for k in (2, 1, 3):
        send(zs.at[m4(z + k)], zr.at[k - 1], zsem, k, (f, m4(z + k)))
    total = zf[z]
    for k in (1, 3, 2):
        arrived(zr.at[k - 1], zsem, k)
        total = total + zr[k - 1].astype(F32)
    zsum[...] = total

    def out_copy(p, to):
        return pltpu.make_async_remote_copy(
            src_ref=zsum.at[pl.ds(pl.multiple_of(to * TOK, TOK), TOK)], dst_ref=comb.at[f],
            send_sem=csem.at[0, p], recv_sem=csem.at[1, p], device_id=(to, z), device_id_type=MESH,
        )

    def out_send(p, carry):
        out_copy(p, lax.rem(f + p, NF)).start()
        return carry

    lax.fori_loop(1, NF, out_send, 0)
    comb[f] = zsum[pl.ds(pl.multiple_of(f * TOK, TOK), TOK), :]

    def out_wait(p, carry):
        src = lax.rem(f - p + NF, NF)
        pltpu.make_async_remote_copy(
            src_ref=comb.at[src], dst_ref=comb.at[src], send_sem=csem.at[0, p], recv_sem=csem.at[1, p],
            device_id=(lax.rem(f + p, NF), z), device_id_type=MESH,
        ).wait_recv()
        out_copy(p, lax.rem(f + p, NF)).wait_send()
        return carry

    lax.fori_loop(1, NF, out_wait, 0)
    for k in range(NF):
        combined[:, k * COLS : (k + 1) * COLS] = comb[k].astype(BF)

    for j in range(CHUNKS):
        for i in range(PER):
            dx, dy = OFFSETS[j][i // 2]
            if (dx, dy) == (0, 0) and i % 2 == 0:
                continue
            src = fid(m4(y - dy), m4(x - dx), lax.rem(c + i % 2, 2))
            arrived(owned.at[0, :, pl.ds(pl.multiple_of(src * COLS, COLS), COLS)], wsem, place(j, i))
    for cp in own_copy:
        cp.wait()
    for cp in pending:
        cp.wait_send()


def local(grad_parts, master, moment_one, moment_two, gate_owned, up_owned, tokens, expert_ids, gate_values, owner_map):
    vmem = pl.BlockSpec(memory_space=pltpu.VMEM)
    hbm = pl.BlockSpec(memory_space=pl.ANY)
    dma = pltpu.SemaphoreType.DMA
    ring = (2, CHUNKS, PER, HALF, COLS)
    return pl.pallas_call(
        kernel,
        out_shape=(
            jax.ShapeDtypeStruct((1, ROWS, D), BF),
            jax.ShapeDtypeStruct((TOK, D), BF),
        ),
        in_specs=[pl.BlockSpec(memory_space=pltpu.SMEM)] + [vmem] * 3 + [hbm] * 6,
        out_specs=(hbm, vmem),
        scratch_shapes=[
            pltpu.SMEM((EXPERTS,), jnp.int32),
            pltpu.VMEM((EXPERTS, ROWS, COLS), F32),
            pltpu.VMEM((EXPERTS, ROWS, COLS), F32),
            pltpu.VMEM((EXPERTS, ROWS, COLS), F32),
            pltpu.VMEM((EXPERTS, ROWS, COLS), F32),
            pltpu.VMEM((3, EXPERTS, ROWS, COLS), F32),
            pltpu.VMEM((2 * ROWS, D), BF),
            pltpu.VMEM((2 * TOK, WIDE), BF),
            pltpu.VMEM((NZ, 2 * TOK, WIDE), BF),
            pltpu.VMEM((NY, NX, NC, NZ * TOK, TCOLS), BF),
            pltpu.VMEM((NY, NX, NC, ROWS, NBLK * SLOTS), BF),
            pltpu.VMEM((NBLK, EXPERTS, BLK), F32),
            pltpu.VMEM((EXPERTS, BLK), F32),
            pltpu.VMEM(ring, BF),
            pltpu.VMEM(ring, BF),
            pltpu.VMEM(ring, BF),
            pltpu.VMEM(ring, BF),
            pltpu.VMEM(ring, BF),
            pltpu.VMEM(ring, BF),
            pltpu.VMEM((EXPERTS, ROWS, COLS), BF),
            pltpu.VMEM((COLS, TOKENS), F32),
            pltpu.VMEM((NZ, TOKENS // NZ, COLS), F32),
            pltpu.VMEM((NZ, TOKENS // NZ, COLS), BF),
            pltpu.VMEM((NZ - 1, TOKENS // NZ, COLS), BF),
            pltpu.VMEM((TOKENS // NZ, COLS), F32),
            pltpu.VMEM((NF, TOK, COLS), F32),
            dma((10,)),
            dma((2, 2 * CHUNKS)),
            dma((2, 2 * CHUNKS)),
            dma((2, 2 * CHUNKS)),
            dma((2, EXPERTS)),
            dma((2, NZ)),
            dma((2, 72)),
            dma((2, 72)),
            dma((2, NZ)),
            dma((2, NF)),
        ],
        compiler_params=pltpu.CompilerParams(
            collective_id=0, has_side_effects=True, vmem_limit_bytes=60 * 2**20
        ),
    )(owner_map, tokens, expert_ids, gate_values, grad_parts, master, moment_one, moment_two, gate_owned, up_owned)


def solution(mesh):
    in_specs = (
        P("dp", None, None, "fsdp"),
        P(None, "dp", "fsdp"),
        P(None, "dp", "fsdp"),
        P(None, "dp", "fsdp"),
        P("fsdp", "dp", None),
        P("fsdp", "dp", None),
        P(("fsdp", "dp"), None),
        P(("fsdp", "dp"), None),
        P(("fsdp", "dp"), None),
        P(),
    )
    out_specs = (P("fsdp", "dp", None), P(("fsdp", "dp"), None))
    return jax.shard_map(local, mesh=mesh, in_specs=in_specs, out_specs=out_specs, check_vma=False)
```
